256 devices in a mesh: img: 8 (over z_hi, x), cap: 16 (over y, z_lo), chip: 2 (over core).
Axes of the slice: x: 4, y: 4, z: 8 (z_hi: 2, z_lo: 4; z = z_hi * 4 + z_lo), core: 2. Of those that a mesh axis runs over, the one named last changes fastest.
Arguments:
- teacher_img: float32 [16, 16, 64, 1280], P(('img', 'chip'), 'cap'), may hold values from -4096 to 4096
- teacher_cap: float32 [16, 16, 64, 1280], P('cap', ('img', 'chip')), may hold values from -4096 to 4096
- student_img: bfloat16 [16, 16, 64, 512], P(('img', 'chip'), 'cap'), may hold values from -4096 to 4096
- student_cap: bfloat16 [16, 16, 64, 512], P('cap', ('img', 'chip')), may hold values from -4096 to 4096
Outputs:
- grad_img: float32 [16, 16, 64, 512], P(('img', 'chip'), 'cap')
- grad_cap: float32 [16, 16, 64, 512], P('cap', ('img', 'chip'))
The draws below stay inside these ranges and needn't reach their ends.
All inputs are finite; a program needn't handle non-finite values.
Results may differ from the reference program's by a relative error of at most 0.0023.
Values may be sent and summed in bfloat16 or wider, within the bound.
No kernel may reach another device: no remote copies, remote signals or barrier semaphores. Data moves between devices by JAX's collectives and lax.ppermute only.
A program may use at most 64 MiB of HBM per device.

```python
import math
import jax
import jax.numpy as jnp
from jax import lax

DT = 1280
DS = 512
ROWS = 1024
PAIRS = 16384
COLS = 1024


def embed_pair(key, width, logit_scale, low, high):
    keys = jax.random.split(key, 6)
    image_rows = jnp.clip(jax.random.normal(keys[0], (PAIRS, width), jnp.float32), -4.0, 4.0)
    image_rows = image_rows * jnp.exp(jax.random.uniform(keys[1], (PAIRS, 1), jnp.float32, math.log(low), math.log(high)))
    caption_rows = jnp.clip(jax.random.normal(keys[2], (PAIRS, width), jnp.float32), -4.0, 4.0)
    caption_rows = caption_rows * jnp.exp(jax.random.uniform(keys[3], (PAIRS, 1), jnp.float32, math.log(low), math.log(high)))
    partner = jnp.roll(image_rows, 7, axis=0)
    position = jnp.arange(PAIRS, dtype=jnp.int32)[:, None]
    chosen = jnp.logical_or(jax.random.randint(keys[4], (PAIRS, 1), 0, 64) == 0, position % 61 == 5)
    leading = chosen.astype(jnp.float32)
    level = jax.random.randint(keys[5], (PAIRS, 1), 0, 3).astype(jnp.float32)
    target = (200.0 + 200.0 * level) / (logit_scale * width) * partner
    follow = jnp.roll(leading, 1, axis=0) * (1.0 - leading)
    nearby = jnp.roll(target, 1, axis=0) * 0.994
    caption_rows = caption_rows * (1.0 - leading - follow) + leading * target + follow * nearby
    blocks = PAIRS // ROWS
    col_blocks = PAIRS // COLS
    image_rows = image_rows.reshape(blocks, col_blocks, ROWS // col_blocks, width)
    caption_rows = caption_rows.reshape(col_blocks, blocks, COLS // blocks, width)
    return (image_rows, caption_rows)


def scale_range():
    return (0.7, 1.6)


def draw_teacher_img(key, part):
    low, high = scale_range()
    return embed_pair(jax.random.fold_in(key, 11), DT, 0.0625, low, high)[0]


def draw_teacher_cap(key, part):
    low, high = scale_range()
    return embed_pair(jax.random.fold_in(key, 11), DT, 0.0625, low, high)[1]


def draw_student_img(key, part):
    low, high = scale_range()
    return embed_pair(jax.random.fold_in(key, 12), DS, 0.125, low, high)[0].astype(jnp.bfloat16)


def draw_student_cap(key, part):
    low, high = scale_range()
    return embed_pair(jax.random.fold_in(key, 12), DS, 0.125, low, high)[1].astype(jnp.bfloat16)


def setup_inputs(seed: int = 0) -> dict:
    splits = jax.random.split(jax.random.key(seed), 5)
    teacher_img = draw_teacher_img(jax.random.fold_in(splits[4], 71), 0)
    teacher_cap = draw_teacher_cap(jax.random.fold_in(splits[4], 71), 0)
    student_img = draw_student_img(jax.random.fold_in(splits[4], 71), 0)
    student_cap = draw_student_cap(jax.random.fold_in(splits[4], 71), 0)
    return {"teacher_img": teacher_img, "teacher_cap": teacher_cap, "student_img": student_img, "student_cap": student_cap}


teacher_scale = 0.0625
student_scale = 0.125


def teacher_block(rows, columns):
    product = lax.dot_general(rows, columns, (((1,), (1,)), ((), ())), precision=lax.Precision.HIGHEST, preferred_element_type=jnp.float32)
    return teacher_scale * product


def student_block(rows, columns):
    product = lax.dot_general(rows, columns, (((1,), (1,)), ((), ())), preferred_element_type=jnp.float32)
    return student_scale * product


def absorb(peak, total, tile):
    new_peak = jnp.maximum(peak, jnp.max(tile, axis=0))
    new_total = total * jnp.exp(peak - new_peak) + jnp.sum(jnp.exp(tile - new_peak[None, :]), axis=0)
    return new_peak, new_total


def reference(teacher_img, teacher_cap, student_img, student_cap):
    blocks = PAIRS // ROWS
    teacher_cap = teacher_cap.reshape(PAIRS, DT)
    student_cap = student_cap.reshape(PAIRS, DS)
    teacher_rows = teacher_img.reshape(blocks, ROWS, DT)
    student_rows = student_img.reshape(blocks, ROWS, DS)

    def first_pass(carry, pieces):
        teacher_piece, student_piece = pieces
        teacher_tile = teacher_block(teacher_piece, teacher_cap)
        student_tile = student_block(student_piece, student_cap)
        teacher_peak, teacher_total = absorb(carry[0], carry[1], teacher_tile)
        student_peak, student_total = absorb(carry[2], carry[3], student_tile)
        row_teacher = jax.nn.logsumexp(teacher_tile, axis=1)
        row_student = jax.nn.logsumexp(student_tile, axis=1)
        return (teacher_peak, teacher_total, student_peak, student_total), (row_teacher, row_student)

    start_peak = jnp.full((PAIRS,), -jnp.inf, jnp.float32)
    start_total = jnp.zeros((PAIRS,), jnp.float32)
    stats, rows_lse = lax.scan(first_pass, (start_peak, start_total, start_peak, start_total), (teacher_rows, student_rows))
    col_teacher = stats[0] + jnp.log(stats[1])
    col_student = stats[2] + jnp.log(stats[3])

    def second_pass(carry, pieces):
        teacher_piece, student_piece, row_teacher, row_student = pieces
        teacher_tile = teacher_block(teacher_piece, teacher_cap)
        student_tile = student_block(student_piece, student_cap)
        along_rows = jnp.exp(student_tile - row_student[:, None]) - jnp.exp(teacher_tile - row_teacher[:, None])
        along_cols = jnp.exp(student_tile - col_student[None, :]) - jnp.exp(teacher_tile - col_teacher[None, :])
        weights = (student_scale * 0.5 * (along_rows + along_cols)).astype(jnp.bfloat16)
        image_piece = jnp.dot(weights, student_cap, preferred_element_type=jnp.float32)
        caption_sum = carry + lax.dot_general(weights, student_piece, (((0,), (0,)), ((), ())), preferred_element_type=jnp.float32)
        return caption_sum, image_piece

    grad_cap, image_blocks = lax.scan(second_pass, jnp.zeros((PAIRS, DS), jnp.float32), (teacher_rows, student_rows, rows_lse[0], rows_lse[1]))
    col_blocks = PAIRS // COLS
    grad_img = image_blocks.reshape(blocks, col_blocks, ROWS // col_blocks, DS)
    grad_cap = grad_cap.reshape(col_blocks, blocks, COLS // blocks, DS)
    return grad_img, grad_cap
```

```python
import jax
import jax.numpy as jnp
from jax import lax
from jax.experimental import pallas as pl
from jax.experimental.pallas import tpu as pltpu
from jax.sharding import Mesh, PartitionSpec as P

teacher_scale = 0.0625
student_scale = 0.125
PLANE = ("x", "y")
RING = ("zh", "zl")
COLUMN = ("zh", "zl", "core")
BF16 = jnp.bfloat16
F32 = jnp.float32
VMEM_LIMIT = 56 * 1024 * 1024


def nt(a, b):
    return lax.dot_general(a, b, (((1,), (1,)), ((), ())), preferred_element_type=F32)


def tn(a, b):
    return lax.dot_general(a, b, (((0,), (0,)), ((), ())), preferred_element_type=F32)


def pack_kernel(ti_ref, tc_ref, si_ref, sc_ref, rows_ref, cols_ref):
    for t_ref, s_ref, o_ref in ((ti_ref, si_ref, rows_ref), (tc_ref, sc_ref, cols_ref)):
        t = t_ref[...]
        width = t.shape[1]
        hi = t.astype(BF16)
        o_ref[:, :width] = hi
        o_ref[:, width : 2 * width] = (t - hi.astype(F32)).astype(BF16)
        o_ref[:, 2 * width :] = s_ref[...]


def pack(ti, tc, si, sc):
    share, width = ti.shape
    total = 2 * width + si.shape[1]
    return pl.pallas_call(
        pack_kernel,
        out_shape=(
            jax.ShapeDtypeStruct((share, total), BF16),
            jax.ShapeDtypeStruct((tc.shape[0], total), BF16),
        ),
        name="pack",
    )(ti, tc, si, sc)


def logits_kernel(width, rows_ref, cols_ref, t_ref, s_ref, row_ref, col_ref):
    step = pl.program_id(0)
    steps = pl.num_programs(0)
    block = cols_ref.shape[0]
    r_hi = rows_ref[:, :width]
    r_lo = rows_ref[:, width : 2 * width]
    c_hi = cols_ref[:, :width]
    c_lo = cols_ref[:, width : 2 * width]
    teacher = teacher_scale * ((nt(r_lo, c_hi) + nt(r_hi, c_lo)) + nt(r_hi, c_hi))
    student = student_scale * nt(rows_ref[:, 2 * width :], cols_ref[:, 2 * width :])
    here = pl.ds(pl.multiple_of(step * block, block), block)
    t_ref[:, here] = teacher
    s_ref[:, here] = student
    for k, tile in enumerate((teacher, student)):
        peak = jnp.max(tile, axis=0, keepdims=True)
        total = jnp.sum(jnp.exp(tile - peak), axis=0, keepdims=True)
        col_ref[k : k + 1, :] = peak + jnp.log(total)

    @pl.when(step == steps - 1)
    def _():
        lanes = lax.broadcasted_iota(jnp.int32, (t_ref.shape[0], 128), 1)
        found = []
        for ref in (t_ref, s_ref):
            tile = ref[...]
            peak = jnp.max(tile, axis=1, keepdims=True)
            total = jnp.sum(jnp.exp(tile - peak), axis=1, keepdims=True)
            found.append(peak + jnp.log(total))
        both = jnp.where(lanes == 0, found[0], found[1])
        row_ref[...] = jnp.transpose(both)[:2, :]


def logits(rows, cols, width):
    m, total = rows.shape
    n = cols.shape[0]
    block = 256
    return pl.pallas_call(
        lambda *refs: logits_kernel(width, *refs),
        grid=(n // block,),
        in_specs=[
            pl.BlockSpec((m, total), lambda i: (0, 0)),
            pl.BlockSpec((block, total), lambda i: (i, 0)),
        ],
        out_specs=[
            pl.BlockSpec((m, n), lambda i: (0, 0)),
            pl.BlockSpec((m, n), lambda i: (0, 0)),
            pl.BlockSpec((2, m), lambda i: (0, 0)),
            pl.BlockSpec((2, block), lambda i: (0, i)),
        ],
        out_shape=[
            jax.ShapeDtypeStruct((m, n), F32),
            jax.ShapeDtypeStruct((m, n), F32),
            jax.ShapeDtypeStruct((2, m), F32),
            jax.ShapeDtypeStruct((2, n), F32),
        ],
        compiler_params=pltpu.CompilerParams(vmem_limit_bytes=VMEM_LIMIT),
        name="logits",
    )(rows, cols)


def join(parts):
    peak = jnp.max(parts, axis=0)
    return peak + jnp.log(jnp.sum(jnp.exp(parts - peak[None]), axis=0))


def grads_kernel(t_ref, s_ref, row_ref, col_ref, srow_ref, scol_ref, img_ref, cap_ref):
    step = pl.program_id(0)
    t = t_ref[...]
    s = s_ref[...]
    lse = row_ref[...]
    along_rows = jnp.exp(s - lse[:, 1:2]) - jnp.exp(t - lse[:, 0:1])
    along_cols = jnp.exp(s - col_ref[1:2, :]) - jnp.exp(t - col_ref[0:1, :])
    weights = (student_scale * 0.5 * (along_rows + along_cols)).astype(BF16)
    img_ref[...] = jnp.dot(weights, scol_ref[...], preferred_element_type=F32).astype(BF16)
    part = tn(weights, srow_ref[...])

    @pl.when(step == 0)
    def _():
        cap_ref[...] = part

    @pl.when(step > 0)
    def _():
        cap_ref[...] += part


def grads(t, s, row_lse, col_lse, rows, cols, width):
    m, n = t.shape
    ds = rows.shape[1] - 2 * width
    at = 2 * width // ds
    block = 256
    return pl.pallas_call(
        grads_kernel,
        grid=(m // block,),
        in_specs=[
            pl.BlockSpec((block, n), lambda i: (i, 0)),
            pl.BlockSpec((block, n), lambda i: (i, 0)),
            pl.BlockSpec((block, 2), lambda i: (i, 0)),
            pl.BlockSpec((2, n), lambda i: (0, 0)),
            pl.BlockSpec((block, ds), lambda i: (i, at)),
            pl.BlockSpec((n, ds), lambda i: (0, at)),
        ],
        out_specs=[
            pl.BlockSpec((block, ds), lambda i: (i, 0)),
            pl.BlockSpec((n, ds), lambda i: (0, 0)),
        ],
        out_shape=[
            jax.ShapeDtypeStruct((m, ds), BF16),
            jax.ShapeDtypeStruct((n, ds), F32),
        ],
        compiler_params=pltpu.CompilerParams(vmem_limit_bytes=VMEM_LIMIT),
        name="grads",
    )(t, s, row_lse, col_lse, rows, cols)


def spread(x, axes):
    n = lax.axis_size(axes)
    return lax.all_to_all(jnp.broadcast_to(x, (n,) + x.shape), axes, 0, 0)


def local(teacher_img, teacher_cap, student_img, student_cap):
    width = teacher_img.shape[3]
    share, ds = student_img.shape[2:]
    plane = lax.axis_size(PLANE)
    ring = lax.axis_size(RING)
    rows_own, cols_own = pack(
        teacher_img[0, 0], teacher_cap[0, 0], student_img[0, 0], student_cap[0, 0]
    )
    rows = lax.all_gather(rows_own, PLANE, axis=0, tiled=True)
    cols = lax.all_gather(cols_own, COLUMN, axis=0, tiled=True)
    t, s, row_part, col_part = logits(rows, cols, width)
    row_lse = join(spread(row_part, PLANE))
    col_lse = join(spread(col_part, COLUMN))
    img_terms, cap_terms = grads(t, s, row_lse.T, col_lse, rows, cols, width)
    core = lax.axis_index("core")
    cap_terms = cap_terms.reshape(ring, 2, share, ds)
    theirs = lax.dynamic_index_in_dim(cap_terms, 1 - core, 1, keepdims=False)
    mine = lax.dynamic_index_in_dim(cap_terms, core, 1, keepdims=False)
    mine = (mine + lax.ppermute(theirs, "core", [(0, 1), (1, 0)])).astype(BF16)
    img_sent = lax.all_to_all(img_terms.reshape(plane, share, ds), PLANE, 0, 0)
    cap_sent = lax.all_to_all(mine, RING, 0, 0)
    grad_img = jnp.sum(img_sent.astype(F32), axis=0)
    grad_cap = jnp.sum(cap_sent.astype(F32), axis=0)
    return grad_img[None, None], grad_cap[None, None]


def solution(mesh):
    fine = Mesh(mesh.devices.reshape(2, 4, 4, 4, 2), ("zh", "x", "y", "zl", "core"))
    img = P(("zh", "x", "core"), ("y", "zl"), None, None)
    cap = P(("y", "zl"), ("zh", "x", "core"), None, None)
    return jax.shard_map(
        local,
        mesh=fine,
        in_specs=(img, cap, img, cap),
        out_specs=(img, cap),
        check_vma=False,
    )
```

```python
import math

import jax
import jax.numpy as jnp
from jax import lax
from jax.experimental import pallas as pl
from jax.experimental.pallas import tpu as pltpu
from jax.sharding import Mesh, PartitionSpec as P

LOG2E = math.log2(math.e)
teacher_scale = 0.0625 * LOG2E
student_scale = 0.125 * LOG2E
weight_scale = 0.125 * 0.5
PLANE = ("x", "y")
RING = ("zh", "zl")
COLUMN = ("zh", "zl", "core")
BF16 = jnp.bfloat16
F32 = jnp.float32
VMEM_LIMIT = 56 * 1024 * 1024
ANY = pl.BlockSpec(memory_space=pl.ANY)
VMEM = pl.BlockSpec(memory_space=pltpu.VMEM)
SMEM = pl.BlockSpec(memory_space=pltpu.SMEM)
PARAMS = pltpu.CompilerParams(vmem_limit_bytes=VMEM_LIMIT)


def nt(a, b):
    return lax.dot_general(a, b, (((1,), (1,)), ((), ())), preferred_element_type=F32)


def tn(a, b):
    return lax.dot_general(a, b, (((0,), (0,)), ((), ())), preferred_element_type=F32)


def log2_sum(tile, axis):
    peak = jnp.max(tile, axis=axis, keepdims=True)
    total = jnp.sum(jnp.exp2(tile - peak), axis=axis, keepdims=True)
    return peak + jnp.log(total) * LOG2E


def join(a, b):
    return jnp.maximum(a, b) + jnp.log1p(jnp.exp2(-jnp.abs(a - b))) * LOG2E


def pack_kernel(ti_ref, tc_ref, si_ref, sc_ref, rows_ref, cols_ref):
    width = ti_ref.shape[1]
    for t_ref, s_ref, o_ref, hi_at in ((ti_ref, si_ref, rows_ref, 0), (tc_ref, sc_ref, cols_ref, 1)):
        t = t_ref[...]
        hi = t.astype(BF16)
        lo_at = 1 - hi_at
        o_ref[:, hi_at * width : (hi_at + 1) * width] = hi
        o_ref[:, lo_at * width : (lo_at + 1) * width] = (t - hi.astype(F32)).astype(BF16)
        o_ref[:, 2 * width :] = s_ref[...]


def pack(ti, tc, si, sc):
    share, width = ti.shape
    total = 2 * width + si.shape[1]
    return pl.pallas_call(
        pack_kernel,
        out_shape=[jax.ShapeDtypeStruct((share, total), BF16)] * 2,
        name="pack",
    )(ti, tc, si, sc)


def logits(place, rows, pieces, width, share, ring, plane):
    m, total = rows.shape
    n = 2 * ring * share
    ds = total - 2 * width
    half = ring // 2
    tile = 256

    def kernel(place_ref, rows_hbm, *rest):
        piece = rest[: 2 * half + 1]
        t_hbm, s_hbm, row_ref, col_ref, scol_ref = rest[2 * half + 1 : 2 * half + 6]
        r_buf, c_buf, t_buf, s_buf, row_sem, col_sem, out_sem = rest[2 * half + 6 :]
        z = place_ref[0]
        sign = place_ref[1]
        row_copy = pltpu.make_async_copy(rows_hbm, r_buf, row_sem)
        row_copy.start()
        plan = []
        for k in range(half):
            at = lax.rem(z + sign * k + ring, ring)
            plan += [(piece[k].at[0], at), (piece[k].at[1], ring + at)]
            if k:
                at = lax.rem(z - sign * k + ring, ring)
                other = piece[half + k - 1]
                plan += [(other.at[1], at), (other.at[0], ring + at)]
        at = lax.rem(z + half, ring)
        plan += [(piece[2 * half - 1], at), (piece[2 * half], ring + at)]
        copies = []
        for i, (src, at) in enumerate(plan):
            there = pl.ds(pl.multiple_of(at * share, share), share)
            copies.append(pltpu.make_async_copy(src, c_buf.at[there], col_sem.at[i]))
            copies[-1].start()
        row_copy.wait()
        for copy in copies:
            copy.wait()
        scol_ref[...] = c_buf[:, 2 * width :]
        outs = []
        for j in range(n // tile):
            here = slice(j * tile, (j + 1) * tile)
            c = c_buf[here, :]
            teacher = teacher_scale * (
                nt(r_buf[:, : 2 * width], c[:, : 2 * width])
                + nt(r_buf[:, :width], c[:, width : 2 * width])
            )
            student = student_scale * nt(r_buf[:, 2 * width :], c[:, 2 * width :])
            for k, (value, buf, hbm) in enumerate(
                ((teacher, t_buf, t_hbm), (student, s_buf, s_hbm))
            ):
                buf[:, here] = value
                copy = pltpu.make_async_copy(
                    buf.at[:, here], hbm.at[:, here], out_sem.at[2 * j + k]
                )
                copy.start()
                outs.append(copy)
                col_ref[k : k + 1, here] = log2_sum(value, 0)
        lanes = lax.broadcasted_iota(jnp.int32, (m, 128), 1)
        both = jnp.where(lanes == 0, log2_sum(t_buf[...], 1), log2_sum(s_buf[...], 1))
        row_ref[...] = jnp.broadcast_to(jnp.transpose(both)[None, :2, :], (plane, 2, m))
        for copy in outs:
            copy.wait()

    return pl.pallas_call(
        kernel,
        in_specs=[SMEM] + [ANY] * (2 * half + 2),
        out_specs=[ANY, ANY, VMEM, VMEM, VMEM],
        out_shape=[
            jax.ShapeDtypeStruct((m, n), F32),
            jax.ShapeDtypeStruct((m, n), F32),
            jax.ShapeDtypeStruct((plane, 2, m), F32),
            jax.ShapeDtypeStruct((2, n), F32),
            jax.ShapeDtypeStruct((n, ds), BF16),
        ],
        scratch_shapes=[
            pltpu.VMEM((m, total), BF16),
            pltpu.VMEM((n, total), BF16),
            pltpu.VMEM((m, n), F32),
            pltpu.VMEM((m, n), F32),
            pltpu.SemaphoreType.DMA,
            pltpu.SemaphoreType.DMA((2 * ring,)),
            pltpu.SemaphoreType.DMA((2 * n // tile,)),
        ],
        compiler_params=PARAMS,
        cost_estimate=pl.CostEstimate(
            flops=2 * m * n * (3 * width + ds),
            bytes_accessed=2 * (m + n) * total + 8 * m * n,
            transcendentals=4 * m * n,
        ),
        name="logits",
    )(place, rows, *pieces)


def weights(t, s, row_parts, col_lse, scol):
    m, n = t.shape
    ds = scol.shape[1]
    plane = row_parts.shape[0]
    block = 512

    def kernel(t_ref, s_ref, parts_ref, col_ref, scol_ref, w_ref, img_ref, lse):
        step = pl.program_id(0)

        @pl.when(step == 0)
        def _():
            parts = parts_ref[...]
            peak = jnp.max(parts, axis=0)
            total = jnp.sum(jnp.exp2(parts - peak[None]), axis=0)
            row = peak + jnp.log(total) * LOG2E
            lse[...] = jnp.transpose(jnp.concatenate([row, jnp.zeros((126, m), F32)], axis=0))

        t = t_ref[...]
        s = s_ref[...]
        row = lse[pl.ds(pl.multiple_of(step * block, block), block), :]
        along_rows = jnp.exp2(s - row[:, 1:2]) - jnp.exp2(t - row[:, 0:1])
        along_cols = jnp.exp2(s - col_ref[1:2, :]) - jnp.exp2(t - col_ref[0:1, :])
        w = (weight_scale * (along_rows + along_cols)).astype(BF16)
        w_ref[...] = w
        img_ref[...] = jnp.dot(w, scol_ref[...], preferred_element_type=F32).astype(BF16)

    return pl.pallas_call(
        kernel,
        grid=(m // block,),
        in_specs=[
            pl.BlockSpec((block, n), lambda i: (i, 0)),
            pl.BlockSpec((block, n), lambda i: (i, 0)),
            pl.BlockSpec((plane, 2, m), lambda i: (0, 0, 0)),
            pl.BlockSpec((2, n), lambda i: (0, 0)),
            pl.BlockSpec((n, ds), lambda i: (0, 0)),
        ],
        out_specs=[
            pl.BlockSpec((block, n), lambda i: (i, 0)),
            pl.BlockSpec((block, ds), lambda i: (i, 0)),
        ],
        out_shape=[
            jax.ShapeDtypeStruct((m, n), BF16),
            jax.ShapeDtypeStruct((m, ds), BF16),
        ],
        scratch_shapes=[pltpu.VMEM((m, 128), F32)],
        compiler_params=PARAMS,
        cost_estimate=pl.CostEstimate(
            flops=2 * m * n * ds, bytes_accessed=10 * m * n, transcendentals=4 * m * n
        ),
        name="weights",
    )(t, s, row_parts, col_lse, scol)


def cap_terms(w, rows, width):
    m, n = w.shape
    ds = rows.shape[1] - 2 * width
    at = 2 * width // ds

    def kernel(w_ref, rows_ref, mine_ref, theirs_ref):
        part = tn(w_ref[...], rows_ref[...])
        step = pl.program_id(0)

        @pl.when(step == 0)
        def _():
            theirs_ref[...] = part

        @pl.when(step == 1)
        def _():
            mine_ref[...] = part

    return pl.pallas_call(
        kernel,
        grid=(2,),
        in_specs=[
            pl.BlockSpec((m, n // 2), lambda i: (0, 1 - i)),
            pl.BlockSpec((m, ds), lambda i: (0, at)),
        ],
        out_specs=[pl.BlockSpec((n // 2, ds), lambda i: (0, 0))] * 2,
        out_shape=[jax.ShapeDtypeStruct((n // 2, ds), F32)] * 2,
        compiler_params=PARAMS,
        cost_estimate=pl.CostEstimate(
            flops=2 * m * n * ds, bytes_accessed=4 * m * n, transcendentals=0
        ),
        name="cap_terms",
    )(w, rows)


def deal(place, mine, came, ring):
    n, ds = mine.shape
    share = n // ring

    def kernel(place_ref, mine_ref, came_ref, own_ref, *out_refs):
        for k in range(ring):
            at = lax.rem(place_ref[0] + k, ring)
            here = pl.ds(pl.multiple_of(at * share, share), share)
            value = mine_ref[here, :] + came_ref[here, :]
            if k:
                out_refs[k - 1][...] = value.astype(BF16)
            else:
                own_ref[...] = value

    return pl.pallas_call(
        kernel,
        in_specs=[SMEM, VMEM, VMEM],
        out_specs=[VMEM] * ring,
        out_shape=[jax.ShapeDtypeStruct((share, ds), F32)]
        + [jax.ShapeDtypeStruct((share, ds), BF16)] * (ring - 1),
        name="deal",
    )(place, mine, came)


def swap(x):
    return lax.ppermute(x, "core", [(0, 1), (1, 0)])


def apart(x, ring, step):
    pairs = [
        (2 * i + c, 2 * ((i + (step, -step)[c]) % ring) + c) for i in range(ring) for c in range(2)
    ]
    return lax.ppermute(x, COLUMN, pairs)


def local(teacher_img, teacher_cap, student_img, student_cap):
    width = teacher_img.shape[3]
    share, ds = student_img.shape[2:]
    plane = lax.axis_size(PLANE)
    ring = lax.axis_size(RING)
    z = lax.axis_index(RING)
    place = jnp.stack([z, 2 * lax.axis_index("core") - 1]).astype(jnp.int32)
    rows_own, cols_own = pack(
        teacher_img[0, 0], teacher_cap[0, 0], student_img[0, 0], student_cap[0, 0]
    )
    rows = lax.all_gather(rows_own, PLANE, axis=0, tiled=True)

    block = jnp.stack([cols_own, swap(cols_own)])
    own, others = [block], []
    for _ in range(1, ring // 2):
        block = apart(block, ring, 1)
        own.append(block)
        others.append(swap(block))
    far = apart(block[0], ring, 1)
    pieces = own + others + [far, swap(far)]

    t, s, row_parts, col_lse, scol = logits(place, rows, pieces, width, share, ring, plane)
    row_parts = lax.all_to_all(row_parts, PLANE, 0, 0)
    came = swap(col_lse)
    half = ring * share
    col_lse = join(col_lse, jnp.concatenate([came[:, half:], came[:, :half]], axis=1))
    for step in (1, 2, 4):
        pairs = [(i, i ^ step) for i in range(ring)]
        col_lse = join(col_lse, lax.ppermute(col_lse, RING, pairs))

    w, img_terms = weights(t, s, row_parts, col_lse, scol)
    img_sent = lax.all_to_all(img_terms.reshape(plane, share, ds), PLANE, 0, 0)
    mine, theirs = cap_terms(w, rows, width)
    own_share, *dealt = deal(place, mine, swap(theirs), ring)
    grad_cap = own_share
    for k in (4, 3, 5, 2, 6, 1, 7):
        pairs = [(i, (i + k) % ring) for i in range(ring)]
        grad_cap = grad_cap + lax.ppermute(dealt[k - 1], RING, pairs).astype(F32)
    grad_img = jnp.sum(img_sent.astype(F32), axis=0)
    return grad_img[None, None], grad_cap[None, None]


def solution(mesh):
    fine = Mesh(mesh.devices.reshape(2, 4, 4, 4, 2), ("zh", "x", "y", "zl", "core"))
    img = P(("zh", "x", "core"), ("y", "zl"), None, None)
    cap = P(("y", "zl"), ("zh", "x", "core"), None, None)
    return jax.shard_map(
        local,
        mesh=fine,
        in_specs=(img, cap, img, cap),
        out_specs=(img, cap),
        check_vma=False,
    )
```

```python
import math

import jax
import jax.numpy as jnp
from jax import lax
from jax.experimental import pallas as pl
from jax.experimental.pallas import tpu as pltpu
from jax.sharding import Mesh, PartitionSpec as P

LOG2E = math.log2(math.e)
teacher_scale = 0.0625 * LOG2E
student_scale = 0.125 * LOG2E
weight_scale = 0.125 * 0.5
PLANE = ("x", "y")
RING = ("zh", "zl")
BF16 = jnp.bfloat16
F32 = jnp.float32
VMEM_LIMIT = 56 * 1024 * 1024
ANY = pl.BlockSpec(memory_space=pl.ANY)
VMEM = pl.BlockSpec(memory_space=pltpu.VMEM)
SMEM = pl.BlockSpec(memory_space=pltpu.SMEM)
PARAMS = pltpu.CompilerParams(vmem_limit_bytes=VMEM_LIMIT)


def nt(a, b):
    return lax.dot_general(a, b, (((1,), (1,)), ((), ())), preferred_element_type=F32)


def tn(a, b):
    return lax.dot_general(a, b, (((0,), (0,)), ((), ())), preferred_element_type=F32)


def log2_sum(tile, axis):
    peak = jnp.max(tile, axis=axis, keepdims=True)
    total = jnp.sum(jnp.exp2(tile - peak), axis=axis, keepdims=True)
    return peak + jnp.log(total) * LOG2E


def join(a, b):
    return jnp.maximum(a, b) + jnp.log1p(jnp.exp2(-jnp.abs(a - b))) * LOG2E


def pack_kernel(ti_ref, tc_ref, si_ref, sc_ref, rows_ref, cols_ref):
    width = ti_ref.shape[1]
    for t_ref, s_ref, o_ref, hi_at in ((ti_ref, si_ref, rows_ref, 0), (tc_ref, sc_ref, cols_ref, 1)):
        t = t_ref[...]
        hi = t.astype(BF16)
        lo_at = 1 - hi_at
        o_ref[:, hi_at * width : (hi_at + 1) * width] = hi
        o_ref[:, lo_at * width : (lo_at + 1) * width] = (t - hi.astype(F32)).astype(BF16)
        o_ref[:, 2 * width :] = s_ref[...]


def pack(ti, tc, si, sc):
    share, width = ti.shape
    total = 2 * width + si.shape[1]
    return pl.pallas_call(
        pack_kernel,
        out_shape=[jax.ShapeDtypeStruct((share, total), BF16)] * 2,
        name="pack",
    )(ti, tc, si, sc)


def row_plan(x, y, sign, share):
    half = share // 2

    def at(p, q, part=0):
        chip_x = lax.rem(x - sign * p + 8, 4)
        chip_y = lax.rem(y - sign * q + 8, 4)
        return (chip_x * 4 + chip_y) * share + part * half

    plan = []

    def add(piece, *parts):
        first = 0
        for p, q, part in parts:
            size = share if part is None else half
            plan.append((piece, first, size, at(p, q, part or 0)))
            first += size

    add(0, (0, 0, None))
    add(1, (1, 0, None))
    add(2, (3, 0, None))
    add(3, (0, 1, None))
    add(4, (0, 3, None))
    add(5, (2, 0, None), (1, 1, 1), (1, 3, 1))
    add(6, (3, 1, 1), (3, 3, 1))
    add(7, (0, 2, None), (1, 1, 0), (3, 1, 0))
    add(8, (1, 3, 0), (3, 3, 0))
    add(9, (2, 1, 1), (2, 3, 1), (1, 2, 1))
    add(10, (3, 2, 1))
    add(11, (1, 2, 0), (3, 2, 0), (2, 1, 0))
    add(12, (2, 3, 0))
    add(13, (2, 2, 1))
    add(14, (2, 2, 0))
    return plan


def col_plan(z, sign, share, ring):
    half = ring // 2
    plan = []
    for k in range(half):
        behind = lax.rem(z - sign * k + ring, ring) * share
        plan += [(k, 0, behind), (k, 1, ring * share + behind)]
        if k:
            ahead = lax.rem(z + sign * k + ring, ring) * share
            plan += [(half + k - 1, 1, ahead), (half + k - 1, 0, ring * share + ahead)]
    far = lax.rem(z + half, ring) * share
    plan += [(2 * half - 1, None, far), (2 * half, None, ring * share + far)]
    return plan


def logits(place, row_pieces, col_pieces, width, share, ring):
    m = 16 * share
    n = 2 * ring * share
    total = row_pieces[0].shape[1]
    ds = total - 2 * width
    tile = 256
    n_rows = len(row_pieces)
    n_cols = len(col_pieces)

    def kernel(place_ref, *rest):
        rows_in = rest[:n_rows]
        cols_in = rest[n_rows : n_rows + n_cols]
        rest = rest[n_rows + n_cols :]
        t_hbm, s_hbm, row_ref, col_ref, srow_ref, scol_ref = rest[:6]
        r_buf, c_buf, t_buf, s_buf, in_sem, out_sem = rest[6:]
        x, y, z, sign = (place_ref[i] for i in range(4))
        copies = []

        def bring(src, buf, at, size):
            there = pl.ds(pl.multiple_of(at, 32), size)
            copy = pltpu.make_async_copy(src, buf.at[there], in_sem.at[len(copies)])
            copy.start()
            copies.append(copy)

        for piece, first, size, at in row_plan(x, y, sign, share):
            bring(rows_in[piece].at[pl.ds(first, size)], r_buf, at, size)
        for piece, part, at in col_plan(z, sign, share, ring):
            src = cols_in[piece] if part is None else cols_in[piece].at[part]
            bring(src, c_buf, at, share)
        for copy in copies:
            copy.wait()
        srow_ref[...] = r_buf[:, 2 * width :]
        scol_ref[...] = c_buf[:, 2 * width :]
        outs = []
        for j in range(n // tile):
            here = slice(j * tile, (j + 1) * tile)
            c = c_buf[here, :]
            teacher = teacher_scale * (
                nt(r_buf[:, : 2 * width], c[:, : 2 * width])
                + nt(r_buf[:, :width], c[:, width : 2 * width])
            )
            student = student_scale * nt(r_buf[:, 2 * width :], c[:, 2 * width :])
            for k, (value, buf, hbm) in enumerate(
                ((teacher, t_buf, t_hbm), (student, s_buf, s_hbm))
            ):
                buf[:, here] = value
                copy = pltpu.make_async_copy(
                    buf.at[:, here], hbm.at[:, here], out_sem.at[2 * j + k]
                )
                copy.start()
                outs.append(copy)
                col_ref[k : k + 1, here] = log2_sum(value, 0)
        lanes = lax.broadcasted_iota(jnp.int32, (m, 128), 1)
        both = jnp.where(lanes == 0, log2_sum(t_buf[...], 1), log2_sum(s_buf[...], 1))
        row_ref[...] = jnp.transpose(both)[:2, :]
        for copy in outs:
            copy.wait()

    return pl.pallas_call(
        kernel,
        in_specs=[SMEM] + [ANY] * (n_rows + n_cols),
        out_specs=[ANY, ANY, VMEM, VMEM, VMEM, VMEM],
        out_shape=[
            jax.ShapeDtypeStruct((m, n), F32),
            jax.ShapeDtypeStruct((m, n), F32),
            jax.ShapeDtypeStruct((2, m), F32),
            jax.ShapeDtypeStruct((2, n), F32),
            jax.ShapeDtypeStruct((m, ds), BF16),
            jax.ShapeDtypeStruct((n, ds), BF16),
        ],
        scratch_shapes=[
            pltpu.VMEM((m, total), BF16),
            pltpu.VMEM((n, total), BF16),
            pltpu.VMEM((m, n), F32),
            pltpu.VMEM((m, n), F32),
            pltpu.SemaphoreType.DMA((48,)),
            pltpu.SemaphoreType.DMA((2 * n // tile,)),
        ],
        compiler_params=PARAMS,
        cost_estimate=pl.CostEstimate(
            flops=2 * m * n * (3 * width + ds),
            bytes_accessed=2 * (m + n) * total + 8 * m * n,
            transcendentals=4 * m * n,
        ),
        name="logits",
    )(place, *row_pieces, *col_pieces)


def weights(place, t, s, row_lse, col_lse, srow, share, ring):
    m, n = t.shape
    ds = srow.shape[1]
    block = 512

    def kernel(
        place_ref, t_ref, s_ref, row_ref, col_ref, srow_ref, w_ref, mine_ref, theirs_ref, lse, acc
    ):
        step = pl.program_id(0)

        @pl.when(step == 0)
        def _():
            lse[...] = jnp.transpose(
                jnp.concatenate([row_ref[...], jnp.zeros((126, m), F32)], axis=0)
            )

        t = t_ref[...]
        s = s_ref[...]
        row = lse[pl.ds(pl.multiple_of(step * block, block), block), :]
        along_rows = jnp.exp2(s - row[:, 1:2]) - jnp.exp2(t - row[:, 0:1])
        along_cols = jnp.exp2(s - col_ref[1:2, :]) - jnp.exp2(t - col_ref[0:1, :])
        w = (weight_scale * (along_rows + along_cols)).astype(BF16)
        w_ref[...] = w
        part = tn(w, srow_ref[...])

        @pl.when(step == 0)
        def _():
            acc[...] = part

        @pl.when(step > 0)
        def _():
            acc[...] += part

        @pl.when(step == pl.num_programs(0) - 1)
        def _():
            z = place_ref[2]
            sign = place_ref[3]

            def terms(ahead, other):
                at = lax.rem(z + ahead + ring, ring) * share + other * ring * share
                return acc[pl.ds(pl.multiple_of(at, share), share), :]

            half = ring // 2
            slots = [(k, h) for k in range(1, half) for h in (0, 1)]
            for i, (k, h) in enumerate(slots):
                here = slice(i * share, (i + 1) * share)
                mine_ref[here, :] = terms(sign * k, h)
                theirs_ref[here, :] = terms(-sign * k, 1 - h)
            for i, k in enumerate((half, 0)):
                here = slice((ring - 2 + i) * share, (ring - 1 + i) * share)
                mine_ref[here, :] = terms(k, 0)
                theirs_ref[here, :] = terms(k, 1)

    return pl.pallas_call(
        kernel,
        grid=(m // block,),
        in_specs=[
            SMEM,
            pl.BlockSpec((block, n), lambda i: (i, 0)),
            pl.BlockSpec((block, n), lambda i: (i, 0)),
            pl.BlockSpec((2, m), lambda i: (0, 0)),
            pl.BlockSpec((2, n), lambda i: (0, 0)),
            pl.BlockSpec((block, ds), lambda i: (i, 0)),
        ],
        out_specs=[
            pl.BlockSpec((block, n), lambda i: (i, 0)),
            pl.BlockSpec((n // 2, ds), lambda i: (0, 0)),
            pl.BlockSpec((n // 2, ds), lambda i: (0, 0)),
        ],
        out_shape=[
            jax.ShapeDtypeStruct((m, n), BF16),
            jax.ShapeDtypeStruct((n // 2, ds), F32),
            jax.ShapeDtypeStruct((n // 2, ds), F32),
        ],
        scratch_shapes=[pltpu.VMEM((m, 128), F32), pltpu.VMEM((n, ds), F32)],
        compiler_params=PARAMS,
        cost_estimate=pl.CostEstimate(
            flops=2 * m * n * ds, bytes_accessed=10 * m * n, transcendentals=4 * m * n
        ),
        name="weights",
    )(place, t, s, row_lse, col_lse, srow)


def img_terms(w, scol):
    m, n = w.shape
    ds = scol.shape[1]
    block = 512

    def kernel(w_ref, scol_ref, img_ref):
        img_ref[...] = jnp.dot(w_ref[...], scol_ref[...], preferred_element_type=F32).astype(BF16)

    return pl.pallas_call(
        kernel,
        grid=(m // block,),
        in_specs=[
            pl.BlockSpec((block, n), lambda i: (i, 0)),
            pl.BlockSpec((n, ds), lambda i: (0, 0)),
        ],
        out_specs=pl.BlockSpec((block, ds), lambda i: (i, 0)),
        out_shape=jax.ShapeDtypeStruct((m, ds), BF16),
        compiler_params=PARAMS,
        cost_estimate=pl.CostEstimate(
            flops=2 * m * n * ds, bytes_accessed=4 * m * n, transcendentals=0
        ),
        name="img_terms",
    )(w, scol)


def deal(mine, came, share, ring):
    ds = mine.shape[1]
    sizes = [2 * share] * (ring // 2 - 1) + [share]

    def kernel(mine_ref, came_ref, *out_refs):
        first = 0
        for size, ref in zip(sizes + [share], out_refs):
            here = slice(first, first + size)
            ref[...] = (mine_ref[here, :] + came_ref[here, :]).astype(ref.dtype)
            first += size

    return pl.pallas_call(
        kernel,
        in_specs=[VMEM, VMEM],
        out_specs=[VMEM] * (len(sizes) + 1),
        out_shape=[jax.ShapeDtypeStruct((size, ds), BF16) for size in sizes]
        + [jax.ShapeDtypeStruct((share, ds), F32)],
        name="deal",
    )(mine, came)


def swap(x):
    return lax.ppermute(x, "core", [(0, 1), (1, 0)])


def turn(x, axis, step):
    n = lax.axis_size(axis)
    axes = (axis if isinstance(axis, tuple) else (axis,)) + ("core",)
    pairs = [(2 * i + c, 2 * ((i + (step, -step)[c]) % n) + c) for i in range(n) for c in (0, 1)]
    return lax.ppermute(x, axes, pairs)


def join_along(x, axis, step):
    n = lax.axis_size(axis)
    return join(x, lax.ppermute(x, axis, [(i, i ^ step) for i in range(n)]))


def gather(r, c, share):
    hold = lax.optimization_barrier
    half = share // 2
    a = lambda v: v[:half]
    b = lambda v: v[half : 2 * half]
    cat = lambda *v: jnp.concatenate(v, axis=0)
    c0 = jnp.stack([c, swap(c)])
    x1, x1r, y1, y1r, c1 = hold(
        (turn(r, "x", 1), turn(r, "x", -1), turn(r, "y", 1), turn(r, "y", -1), turn(c0, RING, 1))
    )
    bx = cat(b(y1), b(y1r))
    ay = cat(a(x1), a(x1r))
    d1, c1 = hold((swap(c1), c1))
    x2, x2r, y2, y2r, c2, d1 = hold(
        (
            turn(cat(x1, bx), "x", 1),
            turn(bx, "x", -1),
            turn(cat(y1, ay), "y", 1),
            turn(ay, "y", -1),
            turn(c1, RING, 1),
            d1,
        )
    )
    d2, c2 = hold((swap(c2), c2))
    x3, x3r, y3, y3r, c3, d2 = hold(
        (
            turn(cat(x2[share:], b(y2)), "x", 1),
            turn(b(y2), "x", -1),
            turn(cat(y2[share:], a(x2)), "y", 1),
            turn(a(x2), "y", -1),
            turn(c2, RING, 1),
            d2,
        )
    )
    x4, y4, c4, d3 = hold(
        (turn(x3[share:], "x", 1), turn(y3[share:], "y", 1), turn(c3[0], RING, 1), swap(c3))
    )
    rows = [r, x1, x1r, y1, y1r, x2, x2r, y2, y2r, x3, x3r, y3, y3r, x4, y4]
    return rows, [c0, c1, c2, c3, d1, d2, d3, c4, swap(c4)]


def local(teacher_img, teacher_cap, student_img, student_cap):
    width = teacher_img.shape[3]
    share, ds = student_img.shape[2:]
    ring = lax.axis_size(RING)
    spot = [lax.axis_index("x"), lax.axis_index("y"), lax.axis_index(RING)]
    place = jnp.stack(spot + [1 - 2 * lax.axis_index("core")]).astype(jnp.int32)
    rows_own, cols_own = pack(
        teacher_img[0, 0], teacher_cap[0, 0], student_img[0, 0], student_cap[0, 0]
    )
    rows, cols = gather(rows_own, cols_own, share)
    t, s, row_lse, col_lse, srow, scol = logits(place, rows, cols, width, share, ring)

    came = swap(col_lse)
    half = ring * share
    col_lse = join(col_lse, jnp.concatenate([came[:, half:], came[:, :half]], axis=1))
    for step in (1, 2, 4):
        col_lse = join_along(col_lse, RING, step)
    for axis in PLANE:
        for step in (1, 3):
            row_lse = join_along(row_lse, axis, step)

    w, mine, theirs = weights(place, t, s, row_lse, col_lse, srow, share, ring)
    img_sent = lax.all_to_all(img_terms(w, scol).reshape(-1, share, ds), PLANE, 0, 0)
    *dealt, own = deal(mine, swap(theirs), share, ring)
    other = None
    for k, terms in enumerate(dealt, 1):
        terms = turn(terms, RING, k).astype(F32)
        own = own + terms[:share]
        if terms.shape[0] > share:
            other = terms[share:] if other is None else other + terms[share:]
    grad_cap = own + swap(other)
    grad_img = jnp.sum(img_sent.astype(F32), axis=0)
    return grad_img[None, None], grad_cap[None, None]


def solution(mesh):
    fine = Mesh(mesh.devices.reshape(2, 4, 4, 4, 2), ("zh", "x", "y", "zl", "core"))
    img = P(("zh", "x", "core"), ("y", "zl"), None, None)
    cap = P(("y", "zl"), ("zh", "x", "core"), None, None)
    return jax.shard_map(
        local,
        mesh=fine,
        in_specs=(img, cap, img, cap),
        out_specs=(img, cap),
        check_vma=False,
    )
```

```python
import math

import jax
import jax.numpy as jnp
from jax import lax
from jax.experimental import pallas as pl
from jax.experimental.pallas import tpu as pltpu
from jax.sharding import Mesh, PartitionSpec as P

LOG2E = math.log2(math.e)
teacher_scale = 0.0625 * LOG2E
student_scale = 0.125 * LOG2E
weight_scale = 0.125 * 0.5
PLANE = ("x", "y")
RING = ("zh", "zl")
BF16 = jnp.bfloat16
F32 = jnp.float32
MIB = 1024 * 1024
VMEM = pl.BlockSpec(memory_space=pltpu.VMEM)


def nt(a, b):
    return lax.dot_general(a, b, (((1,), (1,)), ((), ())), preferred_element_type=F32)


def tn(a, b):
    return lax.dot_general(a, b, (((0,), (0,)), ((), ())), preferred_element_type=F32)


def log2_sum(tile, axis):
    peak = jnp.max(tile, axis=axis, keepdims=True)
    total = jnp.sum(jnp.exp2(tile - peak), axis=axis, keepdims=True)
    return peak + jnp.log(total) * LOG2E


def join(a, b):
    return jnp.maximum(a, b) + jnp.log1p(jnp.exp2(-jnp.abs(a - b))) * LOG2E


def split(t, s, out_ref, order):
    width = t.shape[1]
    hi = t.astype(BF16)
    parts = {"high": hi, "low": (t - hi.astype(F32)).astype(BF16)}
    for i, name in enumerate(order):
        out_ref[:, i * width : (i + 1) * width] = parts[name]
    out_ref[:, 2 * width :] = s


def pack_rows(t, s):
    def kernel(t_ref, s_ref, out_ref):
        split(t_ref[...], s_ref[...], out_ref, ("high", "low"))

    return pl.pallas_call(
        kernel,
        out_shape=jax.ShapeDtypeStruct((t.shape[0], 2 * t.shape[1] + s.shape[1]), BF16),
        compiler_params=pltpu.CompilerParams(vmem_limit_bytes=16 * MIB),
        name="pack_rows",
    )(t, s)


def pack_cols(t, s, t_other, s_other):
    def kernel(t_ref, s_ref, t_other_ref, s_other_ref, out_ref):
        split(t_ref[...], s_ref[...], out_ref.at[0], ("low", "high"))
        split(t_other_ref[...], s_other_ref[...], out_ref.at[1], ("low", "high"))

    return pl.pallas_call(
        kernel,
        out_shape=jax.ShapeDtypeStruct((2, t.shape[0], 2 * t.shape[1] + s.shape[1]), BF16),
        compiler_params=pltpu.CompilerParams(vmem_limit_bytes=16 * MIB),
        name="pack_cols",
    )(t, s, t_other, s_other)


def row_plan(x, y, sign, share):
    half = share // 2

    def at(p, q, part=0):
        chip_x = lax.rem(x - sign * p + 8, 4)
        chip_y = lax.rem(y - sign * q + 8, 4)
        return (chip_x * 4 + chip_y) * share + part * half

    plan = []

    def add(piece, *parts):
        first = 0
        for p, q, part in parts:
            size = share if part is None else half
            plan.append((piece, first, size, at(p, q, part or 0)))
            first += size

    add(0, (0, 0, None))
    add(1, (1, 0, None))
    add(2, (3, 0, None))
    add(3, (0, 1, None))
    add(4, (0, 3, None))
    add(5, (2, 0, None), (1, 1, 1), (1, 3, 1))
    add(6, (3, 1, 1), (3, 3, 1))
    add(7, (0, 2, None), (1, 1, 0), (3, 1, 0))
    add(8, (1, 3, 0), (3, 3, 0))
    add(9, (2, 1, 1), (2, 3, 1), (1, 2, 1))
    add(10, (3, 2, 1))
    add(11, (1, 2, 0), (3, 2, 0), (2, 1, 0))
    add(12, (2, 3, 0))
    add(13, (2, 2, 1))
    add(14, (2, 2, 0))
    return plan


def col_plan(z, sign, share, ring):
    half = ring // 2
    plan = []
    for k in range(half):
        behind = lax.rem(z - sign * k + ring, ring) * share
        plan += [(k, 0, behind), (k, 1, ring * share + behind)]
        if k:
            ahead = lax.rem(z + sign * k + ring, ring) * share
            plan += [(half + k - 1, 1, ahead), (half + k - 1, 0, ring * share + ahead)]
    far = lax.rem(z + half, ring) * share
    plan += [(2 * half - 1, None, far), (2 * half, None, ring * share + far)]
    return plan


def logits(row_pieces, col_pieces, width, share, ring):
    m = 16 * share
    n = 2 * ring * share
    total = row_pieces[0].shape[1]
    ds = total - 2 * width
    tile = 256
    n_rows = len(row_pieces)
    n_cols = len(col_pieces)

    def kernel(*refs):
        rows_in = refs[:n_rows]
        cols_in = refs[n_rows : n_rows + n_cols]
        refs = refs[n_rows + n_cols :]
        t_ref, s_ref, row_ref, col_ref, srow_ref, scol_ref, r_buf, c_buf = refs
        x, y, z = lax.axis_index("x"), lax.axis_index("y"), lax.axis_index(RING)
        sign = 1 - 2 * lax.axis_index("core")

        def place(src, first, buf, at, size):
            def some_rows(i, _):
                there = pl.ds(pl.multiple_of(at + 16 * i, 16), 16)
                buf[there, :] = src[pl.ds(pl.multiple_of(first + 16 * i, 16), 16), :]
                return 0

            lax.fori_loop(0, size // 16, some_rows, 0)

        for piece, first, size, at in row_plan(x, y, sign, share):
            place(rows_in[piece], first, r_buf, at, size)
        for piece, part, at in col_plan(z, sign, share, ring):
            place(cols_in[piece] if part is None else cols_in[piece].at[part], 0, c_buf, at, share)

        def columns(j, _):
            here = pl.ds(pl.multiple_of(j * tile, tile), tile)
            teacher = teacher_scale * (
                nt(r_buf[:, : 2 * width], c_buf[here, : 2 * width])
                + nt(r_buf[:, :width], c_buf[here, width : 2 * width])
            )
            student = student_scale * nt(r_buf[:, 2 * width :], c_buf[here, 2 * width :])
            for k, (value, ref) in enumerate(((teacher, t_ref), (student, s_ref))):
                ref[:, here] = value
                col_ref[k : k + 1, here] = log2_sum(value, 0)
            return 0

        lax.fori_loop(0, n // tile, columns, 0)
        lanes = lax.broadcasted_iota(jnp.int32, (128, 128), 1)

        def row_sums(i, _):
            here = pl.ds(pl.multiple_of(i * 128, 128), 128)
            teacher = log2_sum(t_ref[here, :], 1)
            student = log2_sum(s_ref[here, :], 1)
            both = jnp.transpose(jnp.where(lanes == 0, teacher, student))
            row_ref[:, here] = both[:2, :]
            srow_ref[here, :] = r_buf[here, 2 * width :]
            scol_ref[here, :] = c_buf[here, 2 * width :]
            return 0

        lax.fori_loop(0, m // 128, row_sums, 0)

    return pl.pallas_call(
        kernel,
        in_specs=[VMEM] * (n_rows + n_cols),
        out_specs=[VMEM] * 6,
        out_shape=[
            jax.ShapeDtypeStruct((m, n), F32),
            jax.ShapeDtypeStruct((m, n), F32),
            jax.ShapeDtypeStruct((2, m), F32),
            jax.ShapeDtypeStruct((2, n), F32),
            jax.ShapeDtypeStruct((m, ds), BF16),
            jax.ShapeDtypeStruct((n, ds), BF16),
        ],
        scratch_shapes=[
            pltpu.VMEM((m, total), BF16),
            pltpu.VMEM((n, total), BF16),
        ],
        compiler_params=pltpu.CompilerParams(vmem_limit_bytes=28 * MIB),
        cost_estimate=pl.CostEstimate(
            flops=2 * m * n * (3 * width + ds),
            bytes_accessed=2 * (m + n) * total + 8 * m * n,
            transcendentals=4 * m * n,
        ),
        name="logits",
    )(*row_pieces, *col_pieces)


def weights(t, s, row_lse, col_lse, srow, share, ring):
    m, n = t.shape
    ds = srow.shape[1]
    block = 512

    def kernel(
        t_ref, s_ref, row_ref, col_ref, srow_ref, w_ref, mine_ref, theirs_ref, lse, acc
    ):
        step = pl.program_id(0)

        @pl.when(step == 0)
        def _():
            lse[...] = jnp.transpose(
                jnp.concatenate([row_ref[...], jnp.zeros((126, m), F32)], axis=0)
            )

        t = t_ref[...]
        s = s_ref[...]
        row = lse[pl.ds(pl.multiple_of(step * block, block), block), :]
        along_rows = jnp.exp2(s - row[:, 1:2]) - jnp.exp2(t - row[:, 0:1])
        along_cols = jnp.exp2(s - col_ref[1:2, :]) - jnp.exp2(t - col_ref[0:1, :])
        w = (weight_scale * (along_rows + along_cols)).astype(BF16)
        w_ref[...] = w
        part = tn(w, srow_ref[...])

        @pl.when(step == 0)
        def _():
            acc[...] = part

        @pl.when(step > 0)
        def _():
            acc[...] += part

        @pl.when(step == pl.num_programs(0) - 1)
        def _():
            z = lax.axis_index(RING)
            sign = 1 - 2 * lax.axis_index("core")

            def terms(ahead, other):
                at = lax.rem(z + ahead + ring, ring) * share + other * ring * share
                return acc[pl.ds(pl.multiple_of(at, share), share), :]

            half = ring // 2
            slots = [(k, h) for k in range(1, half) for h in (0, 1)]
            for i, (k, h) in enumerate(slots):
                here = slice(i * share, (i + 1) * share)
                mine_ref[here, :] = terms(sign * k, h)
                theirs_ref[here, :] = terms(-sign * k, 1 - h)
            for i, k in enumerate((half, 0)):
                here = slice((ring - 2 + i) * share, (ring - 1 + i) * share)
                mine_ref[here, :] = terms(k, 0)
                theirs_ref[here, :] = terms(k, 1)

    return pl.pallas_call(
        kernel,
        grid=(m // block,),
        in_specs=[
            pl.BlockSpec((block, n), lambda i: (i, 0)),
            pl.BlockSpec((block, n), lambda i: (i, 0)),
            pl.BlockSpec((2, m), lambda i: (0, 0)),
            pl.BlockSpec((2, n), lambda i: (0, 0)),
            pl.BlockSpec((block, ds), lambda i: (i, 0)),
        ],
        out_specs=[
            pl.BlockSpec((block, n), lambda i: (i, 0)),
            pl.BlockSpec((n // 2, ds), lambda i: (0, 0)),
            pl.BlockSpec((n // 2, ds), lambda i: (0, 0)),
        ],
        out_shape=[
            jax.ShapeDtypeStruct((m, n), BF16),
            jax.ShapeDtypeStruct((n // 2, ds), F32),
            jax.ShapeDtypeStruct((n // 2, ds), F32),
        ],
        scratch_shapes=[pltpu.VMEM((m, 128), F32), pltpu.VMEM((n, ds), F32)],
        compiler_params=pltpu.CompilerParams(vmem_limit_bytes=20 * MIB),
        cost_estimate=pl.CostEstimate(
            flops=2 * m * n * ds, bytes_accessed=10 * m * n, transcendentals=4 * m * n
        ),
        name="weights",
    )(t, s, row_lse, col_lse, srow)


def img_terms(w, scol):
    m, n = w.shape
    ds = scol.shape[1]
    block = 512

    def kernel(w_ref, scol_ref, img_ref):
        img_ref[...] = jnp.dot(w_ref[...], scol_ref[...], preferred_element_type=F32).astype(BF16)

    return pl.pallas_call(
        kernel,
        grid=(m // block,),
        in_specs=[
            pl.BlockSpec((block, n), lambda i: (i, 0)),
            pl.BlockSpec((n, ds), lambda i: (0, 0)),
        ],
        out_specs=pl.BlockSpec((block, ds), lambda i: (i, 0)),
        out_shape=jax.ShapeDtypeStruct((m, ds), BF16),
        compiler_params=pltpu.CompilerParams(vmem_limit_bytes=10 * MIB),
        cost_estimate=pl.CostEstimate(
            flops=2 * m * n * ds, bytes_accessed=4 * m * n, transcendentals=0
        ),
        name="img_terms",
    )(w, scol)


def deal(mine, came, share, ring):
    ds = mine.shape[1]
    sizes = [2 * share] * (ring // 2 - 1) + [share]

    def kernel(mine_ref, came_ref, *out_refs):
        first = 0
        for size, ref in zip(sizes + [share], out_refs):
            here = slice(first, first + size)
            ref[...] = (mine_ref[here, :] + came_ref[here, :]).astype(ref.dtype)
            first += size

    return pl.pallas_call(
        kernel,
        in_specs=[VMEM, VMEM],
        out_specs=[VMEM] * (len(sizes) + 1),
        out_shape=[jax.ShapeDtypeStruct((size, ds), BF16) for size in sizes]
        + [jax.ShapeDtypeStruct((share, ds), F32)],
        compiler_params=pltpu.CompilerParams(vmem_limit_bytes=10 * MIB),
        name="deal",
    )(mine, came)


def swap(x):
    return lax.ppermute(x, "core", [(0, 1), (1, 0)])


def turn(x, axis, step):
    n = lax.axis_size(axis)
    axes = (axis if isinstance(axis, tuple) else (axis,)) + ("core",)
    pairs = [(2 * i + c, 2 * ((i + (step, -step)[c]) % n) + c) for i in range(n) for c in (0, 1)]
    return lax.ppermute(x, axes, pairs)


def join_along(x, axis, step):
    n = lax.axis_size(axis)
    return join(x, lax.ppermute(x, axis, [(i, i ^ step) for i in range(n)]))


def gather(r, c0, share):
    hold = lax.optimization_barrier
    half = share // 2
    a = lambda v: v[:half]
    b = lambda v: v[half : 2 * half]
    cat = lambda *v: jnp.concatenate(v, axis=0)
    x1, x1r, y1, y1r, c1 = hold(
        (turn(r, "x", 1), turn(r, "x", -1), turn(r, "y", 1), turn(r, "y", -1), turn(c0, RING, 1))
    )
    bx = cat(b(y1), b(y1r))
    ay = cat(a(x1), a(x1r))
    d1, c1 = hold((swap(c1), c1))
    x2, x2r, y2, y2r, c2, d1 = hold(
        (
            turn(cat(x1, bx), "x", 1),
            turn(bx, "x", -1),
            turn(cat(y1, ay), "y", 1),
            turn(ay, "y", -1),
            turn(c1, RING, 1),
            d1,
        )
    )
    x3, x3r, y3, y3r, c3 = hold(
        (
            turn(cat(x2[share:], b(y2)), "x", 1),
            turn(b(y2), "x", -1),
            turn(cat(y2[share:], a(x2)), "y", 1),
            turn(a(x2), "y", -1),
            turn(c2, RING, 1),
        )
    )
    x4, y4, c4, d2, c3 = hold(
        (turn(x3[share:], "x", 1), turn(y3[share:], "y", 1), turn(c3[0], RING, 1), swap(c2), c3)
    )
    rows = [r, x1, x1r, y1, y1r, x2, x2r, y2, y2r, x3, x3r, y3, y3r, x4, y4]
    return rows, [c0, c1, c2, c3, d1, d2, swap(c3), c4, swap(c4)]


def local(teacher_img, teacher_cap, student_img, student_cap):
    width = teacher_img.shape[3]
    share, ds = student_img.shape[2:]
    ring = lax.axis_size(RING)
    rows_own = pack_rows(teacher_img[0, 0], student_img[0, 0])
    cols_own = (teacher_cap[0, 0], student_cap[0, 0])
    cols_pair = pack_cols(*cols_own, *[swap(v) for v in cols_own])
    rows, cols = gather(rows_own, cols_pair, share)
    t, s, row_lse, col_lse, srow, scol = logits(rows, cols, width, share, ring)

    came = swap(col_lse)
    half = ring * share
    col_lse = join(col_lse, jnp.concatenate([came[:, half:], came[:, :half]], axis=1))
    for step in (1, 2, 4):
        col_lse = join_along(col_lse, RING, step)
    for axis in PLANE:
        for step in (1, 3):
            row_lse = join_along(row_lse, axis, step)

    w, mine, theirs = weights(t, s, row_lse, col_lse, srow, share, ring)
    img_sent = lax.all_to_all(img_terms(w, scol).reshape(-1, share, ds), PLANE, 0, 0)
    *dealt, own = deal(mine, swap(theirs), share, ring)
    other = None
    for k, terms in enumerate(dealt, 1):
        terms = turn(terms, RING, k).astype(F32)
        own = own + terms[:share]
        if terms.shape[0] > share:
            other = terms[share:] if other is None else other + terms[share:]
    grad_cap = own + swap(other)
    grad_img = jnp.sum(img_sent.astype(F32), axis=0)
    return grad_img[None, None], grad_cap[None, None]


def solution(mesh):
    fine = Mesh(mesh.devices.reshape(2, 4, 4, 4, 2), ("zh", "x", "y", "zl", "core"))
    img = P(("zh", "x", "core"), ("y", "zl"), None, None)
    cap = P(("y", "zl"), ("zh", "x", "core"), None, None)
    return jax.shard_map(
        local,
        mesh=fine,
        in_specs=(img, cap, img, cap),
        out_specs=(img, cap),
        check_vma=False,
    )
```

```python
import math

import jax
import jax.numpy as jnp
from jax import lax
from jax.experimental import pallas as pl
from jax.experimental.pallas import tpu as pltpu
from jax.sharding import Mesh, PartitionSpec as P

LOG2E = math.log2(math.e)
teacher_scale = 0.0625 * LOG2E
student_scale = 0.125 * LOG2E
weight_scale = 0.125 * 0.5
PLANE = ("x", "y")
RING = ("zh", "zl")
BF16 = jnp.bfloat16
F32 = jnp.float32
MIB = 1024 * 1024
VMEM = pl.BlockSpec(memory_space=pltpu.VMEM)


def nt(a, b):
    return lax.dot_general(a, b, (((1,), (1,)), ((), ())), preferred_element_type=F32)


def tn(a, b):
    return lax.dot_general(a, b, (((0,), (0,)), ((), ())), preferred_element_type=F32)


def log2_sum(tile, axis):
    peak = jnp.max(tile, axis=axis, keepdims=True)
    total = jnp.sum(jnp.exp2(tile - peak), axis=axis, keepdims=True)
    return peak + jnp.log(total) * LOG2E


def join(a, b):
    return jnp.maximum(a, b) + jnp.log1p(jnp.exp2(-jnp.abs(a - b))) * LOG2E


def split(t, s, out_ref, order):
    width = t.shape[1]
    hi = t.astype(BF16)
    parts = {"high": hi, "low": (t - hi.astype(F32)).astype(BF16)}
    for i, name in enumerate(order):
        out_ref[:, i * width : (i + 1) * width] = parts[name]
    out_ref[:, 2 * width :] = s


def pack(*shards):
    share, width = shards[0].shape
    total = 2 * width + shards[1].shape[1]

    def kernel(*refs):
        sources, (rows_ref, cols_ref), (*bufs, sem) = refs[:4], refs[4:6], refs[6:]
        copies = [
            pltpu.make_async_copy(src, buf, sem.at[i])
            for i, (src, buf) in enumerate(zip(sources, bufs))
        ]
        for copy in copies:
            copy.start()
        for copy in copies:
            copy.wait()
        split(bufs[0][...], bufs[1][...], rows_ref, ("high", "low"))
        split(bufs[2][...], bufs[3][...], cols_ref, ("low", "high"))

    return pl.pallas_call(
        kernel,
        in_specs=[pl.BlockSpec(memory_space=pltpu.HBM)] * 4,
        out_specs=[VMEM] * 2,
        out_shape=[jax.ShapeDtypeStruct((share, total), BF16)] * 2,
        scratch_shapes=[pltpu.VMEM(v.shape, v.dtype) for v in shards]
        + [pltpu.SemaphoreType.DMA((4,))],
        compiler_params=pltpu.CompilerParams(vmem_limit_bytes=63 * MIB),
        name="pack",
    )(*shards)


def pair(cols, t_other, s_other):
    def kernel(cols_ref, t_ref, s_ref, out_ref):
        out_ref[0] = cols_ref[...]
        split(t_ref[...], s_ref[...], out_ref.at[1], ("low", "high"))

    return pl.pallas_call(
        kernel,
        out_shape=jax.ShapeDtypeStruct((2,) + cols.shape, BF16),
        compiler_params=pltpu.CompilerParams(vmem_limit_bytes=16 * MIB),
        name="pair",
    )(cols, t_other, s_other)


def row_plan(x, y, sign, share):
    half = share // 2

    def at(p, q, part=0):
        chip_x = lax.rem(x - sign * p + 8, 4)
        chip_y = lax.rem(y - sign * q + 8, 4)
        return (chip_x * 4 + chip_y) * share + part * half

    plan = []

    def add(piece, *parts):
        first = 0
        for p, q, part in parts:
            size = share if part is None else half
            plan.append((piece, first, size, at(p, q, part or 0)))
            first += size

    add(0, (0, 0, None))
    add(1, (1, 0, None))
    add(2, (3, 0, None))
    add(3, (0, 1, None))
    add(4, (0, 3, None))
    add(5, (2, 0, None), (1, 1, 1), (1, 3, 1))
    add(6, (3, 1, 1), (3, 3, 1))
    add(7, (0, 2, None), (1, 1, 0), (3, 1, 0))
    add(8, (1, 3, 0), (3, 3, 0))
    add(9, (2, 1, 1), (2, 3, 1), (1, 2, 1))
    add(10, (3, 2, 1))
    add(11, (1, 2, 0), (3, 2, 0), (2, 1, 0))
    add(12, (2, 3, 0))
    add(13, (2, 2, 1))
    add(14, (2, 2, 0))
    return plan


def col_plan(z, sign, share, ring):
    half = ring // 2
    plan = []
    for k in range(half):
        behind = lax.rem(z - sign * k + ring, ring) * share
        plan += [(k, 0, behind), (k, 1, ring * share + behind)]
        if k:
            ahead = lax.rem(z + sign * k + ring, ring) * share
            plan += [(half + k - 1, 1, ahead), (half + k - 1, 0, ring * share + ahead)]
    far = lax.rem(z + half, ring) * share
    plan += [(2 * half - 1, None, far), (2 * half, None, ring * share + far)]
    return plan


def logits(row_pieces, col_pieces, width, share, ring):
    m = 16 * share
    n = 2 * ring * share
    total = row_pieces[0].shape[1]
    ds = total - 2 * width
    tile = 256
    n_rows = len(row_pieces)
    n_cols = len(col_pieces)

    def kernel(*refs):
        rows_in = refs[:n_rows]
        cols_in = refs[n_rows : n_rows + n_cols]
        refs = refs[n_rows + n_cols :]
        t_ref, s_ref, row_ref, col_ref, srow_ref, scol_ref, r_buf, c_buf = refs
        x, y, z = lax.axis_index("x"), lax.axis_index("y"), lax.axis_index(RING)
        sign = 1 - 2 * lax.axis_index("core")

        def place(src, first, buf, at, size):
            def some_rows(i, _):
                there = pl.ds(pl.multiple_of(at + 32 * i, 32), 32)
                buf[there, :] = src[pl.ds(pl.multiple_of(first + 32 * i, 32), 32), :]
                return 0

            lax.fori_loop(0, size // 32, some_rows, 0)

        for piece, first, size, at in row_plan(x, y, sign, share):
            place(rows_in[piece], first, r_buf, at, size)
        for piece, part, at in col_plan(z, sign, share, ring):
            place(cols_in[piece] if part is None else cols_in[piece].at[part], 0, c_buf, at, share)

        def columns(j, _):
            here = pl.ds(pl.multiple_of(j * tile, tile), tile)
            teacher = teacher_scale * (
                nt(r_buf[:, : 2 * width], c_buf[here, : 2 * width])
                + nt(r_buf[:, :width], c_buf[here, width : 2 * width])
            )
            student = student_scale * nt(r_buf[:, 2 * width :], c_buf[here, 2 * width :])
            for k, (value, ref) in enumerate(((teacher, t_ref), (student, s_ref))):
                ref[:, here] = value
                col_ref[k : k + 1, here] = log2_sum(value, 0)
            return 0

        lax.fori_loop(0, n // tile, columns, 0)
        lanes = lax.broadcasted_iota(jnp.int32, (128, 128), 1)

        def row_sums(i, _):
            here = pl.ds(pl.multiple_of(i * 128, 128), 128)
            teacher = log2_sum(t_ref[here, :], 1)
            student = log2_sum(s_ref[here, :], 1)
            both = jnp.transpose(jnp.where(lanes == 0, teacher, student))
            row_ref[:, here] = both[:2, :]
            srow_ref[here, :] = r_buf[here, 2 * width :]
            scol_ref[here, :] = c_buf[here, 2 * width :]
            return 0

        lax.fori_loop(0, m // 128, row_sums, 0)

    return pl.pallas_call(
        kernel,
        in_specs=[VMEM] * (n_rows + n_cols),
        out_specs=[VMEM] * 6,
        out_shape=[
            jax.ShapeDtypeStruct((m, n), F32),
            jax.ShapeDtypeStruct((m, n), F32),
            jax.ShapeDtypeStruct((2, m), F32),
            jax.ShapeDtypeStruct((2, n), F32),
            jax.ShapeDtypeStruct((m, ds), BF16),
            jax.ShapeDtypeStruct((n, ds), BF16),
        ],
        scratch_shapes=[
            pltpu.VMEM((m, total), BF16),
            pltpu.VMEM((n, total), BF16),
        ],
        compiler_params=pltpu.CompilerParams(vmem_limit_bytes=28 * MIB),
        cost_estimate=pl.CostEstimate(
            flops=2 * m * n * (3 * width + ds),
            bytes_accessed=2 * (m + n) * total + 8 * m * n,
            transcendentals=4 * m * n,
        ),
        name="logits",
    )(*row_pieces, *col_pieces)


def weights(t, s, row_lse, col_lse, srow, scol, share, ring):
    m, n = t.shape
    ds = srow.shape[1]
    block = 512

    def kernel(
        t_ref, s_ref, row_ref, col_ref, srow_ref, scol_ref, img_ref, mine_ref, theirs_ref, lse, acc
    ):
        step = pl.program_id(0)

        @pl.when(step == 0)
        def _():
            lse[...] = jnp.transpose(
                jnp.concatenate([row_ref[...], jnp.zeros((126, m), F32)], axis=0)
            )

        t = t_ref[...]
        s = s_ref[...]
        row = lse[pl.ds(pl.multiple_of(step * block, block), block), :]
        along_rows = jnp.exp2(s - row[:, 1:2]) - jnp.exp2(t - row[:, 0:1])
        along_cols = jnp.exp2(s - col_ref[1:2, :]) - jnp.exp2(t - col_ref[0:1, :])
        w = (weight_scale * (along_rows + along_cols)).astype(BF16)
        part = tn(w, srow_ref[...])
        img_ref[...] = jnp.dot(w, scol_ref[...], preferred_element_type=F32).astype(BF16)

        @pl.when(step == 0)
        def _():
            acc[...] = part

        @pl.when(step > 0)
        def _():
            acc[...] += part

        @pl.when(step == pl.num_programs(0) - 1)
        def _():
            z = lax.axis_index(RING)
            sign = 1 - 2 * lax.axis_index("core")

            def terms(ahead, other):
                at = lax.rem(z + ahead + ring, ring) * share + other * ring * share
                return acc[pl.ds(pl.multiple_of(at, share), share), :]

            half = ring // 2
            slots = [(k, h) for k in range(1, half) for h in (0, 1)]
            for i, (k, h) in enumerate(slots):
                here = slice(i * share, (i + 1) * share)
                mine_ref[here, :] = terms(sign * k, h)
                theirs_ref[here, :] = terms(-sign * k, 1 - h)
            for i, k in enumerate((half, 0)):
                here = slice((ring - 2 + i) * share, (ring - 1 + i) * share)
                mine_ref[here, :] = terms(k, 0)
                theirs_ref[here, :] = terms(k, 1)

    return pl.pallas_call(
        kernel,
        grid=(m // block,),
        in_specs=[
            pl.BlockSpec((block, n), lambda i: (i, 0)),
            pl.BlockSpec((block, n), lambda i: (i, 0)),
            pl.BlockSpec((2, m), lambda i: (0, 0)),
            pl.BlockSpec((2, n), lambda i: (0, 0)),
            pl.BlockSpec((block, ds), lambda i: (i, 0)),
            pl.BlockSpec((n, ds), lambda i: (0, 0)),
        ],
        out_specs=[
            pl.BlockSpec((block, ds), lambda i: (i, 0)),
            pl.BlockSpec((n // 2, ds), lambda i: (0, 0)),
            pl.BlockSpec((n // 2, ds), lambda i: (0, 0)),
        ],
        out_shape=[
            jax.ShapeDtypeStruct((m, ds), BF16),
            jax.ShapeDtypeStruct((n // 2, ds), F32),
            jax.ShapeDtypeStruct((n // 2, ds), F32),
        ],
        scratch_shapes=[pltpu.VMEM((m, 128), F32), pltpu.VMEM((n, ds), F32)],
        compiler_params=pltpu.CompilerParams(vmem_limit_bytes=20 * MIB),
        cost_estimate=pl.CostEstimate(
            flops=4 * m * n * ds, bytes_accessed=10 * m * n, transcendentals=4 * m * n
        ),
        name="weights",
    )(t, s, row_lse, col_lse, srow, scol)


def add_up(terms):
    def kernel(terms_ref, out_ref):
        out_ref[...] = jnp.sum(terms_ref[...].astype(F32), axis=0)

    return pl.pallas_call(
        kernel,
        out_shape=jax.ShapeDtypeStruct(terms.shape[1:], F32),
        compiler_params=pltpu.CompilerParams(vmem_limit_bytes=10 * MIB),
        name="add_up",
    )(terms)


def deal(mine, came, share, ring):
    ds = mine.shape[1]
    sizes = [2 * share] * (ring // 2 - 1) + [share]

    def kernel(mine_ref, came_ref, *out_refs):
        first = 0
        for size, ref in zip(sizes + [share], out_refs):
            here = slice(first, first + size)
            ref[...] = (mine_ref[here, :] + came_ref[here, :]).astype(ref.dtype)
            first += size

    return pl.pallas_call(
        kernel,
        in_specs=[VMEM, VMEM],
        out_specs=[VMEM] * (len(sizes) + 1),
        out_shape=[jax.ShapeDtypeStruct((size, ds), BF16) for size in sizes]
        + [jax.ShapeDtypeStruct((share, ds), F32)],
        compiler_params=pltpu.CompilerParams(vmem_limit_bytes=10 * MIB),
        name="deal",
    )(mine, came)


def swap(x):
    return lax.ppermute(x, "core", [(0, 1), (1, 0)])


def turn(x, axis, step):
    n = lax.axis_size(axis)
    axes = (axis if isinstance(axis, tuple) else (axis,)) + ("core",)
    pairs = [(2 * i + c, 2 * ((i + (step, -step)[c]) % n) + c) for i in range(n) for c in (0, 1)]
    return lax.ppermute(x, axes, pairs)


def join_along(x, axis, step):
    n = lax.axis_size(axis)
    return join(x, lax.ppermute(x, axis, [(i, i ^ step) for i in range(n)]))


def gather(r, c0, share):
    hold = lax.optimization_barrier
    half = share // 2
    a = lambda v: v[:half]
    b = lambda v: v[half : 2 * half]
    cat = lambda *v: jnp.concatenate(v, axis=0)
    x1, x1r, y1, y1r, c1 = hold(
        (turn(r, "x", 1), turn(r, "x", -1), turn(r, "y", 1), turn(r, "y", -1), turn(c0, RING, 1))
    )
    bx = cat(b(y1), b(y1r))
    ay = cat(a(x1), a(x1r))
    d1, c1 = hold((swap(c1), c1))
    x2, x2r, y2, y2r, c2, d1 = hold(
        (
            turn(cat(x1, bx), "x", 1),
            turn(bx, "x", -1),
            turn(cat(y1, ay), "y", 1),
            turn(ay, "y", -1),
            turn(c1, RING, 1),
            d1,
        )
    )
    x3, x3r, y3, y3r, c3 = hold(
        (
            turn(cat(x2[share:], b(y2)), "x", 1),
            turn(b(y2), "x", -1),
            turn(cat(y2[share:], a(x2)), "y", 1),
            turn(a(x2), "y", -1),
            turn(c2, RING, 1),
        )
    )
    x4, y4, c4, d2, d3 = hold(
        (
            turn(x3[share:], "x", 1),
            turn(y3[share:], "y", 1),
            turn(c3[0], RING, 1),
            swap(c2),
            swap(c3),
        )
    )
    rows = [r, x1, x1r, y1, y1r, x2, x2r, y2, y2r, x3, x3r, y3, y3r, x4, y4]
    return rows, [c0, c1, c2, c3, d1, d2, d3, c4, swap(c4)]


def local(teacher_img, teacher_cap, student_img, student_cap):
    width = teacher_img.shape[3]
    share, ds = student_img.shape[2:]
    ring = lax.axis_size(RING)
    came = swap(teacher_cap[0, 0]), swap(student_cap[0, 0])
    rows_own, cols_own = pack(
        teacher_img[0, 0], student_img[0, 0], teacher_cap[0, 0], student_cap[0, 0]
    )
    cols_pair = pair(cols_own, *came)
    rows, cols = gather(rows_own, cols_pair, share)
    t, s, row_lse, col_lse, srow, scol = logits(rows, cols, width, share, ring)

    came = swap(col_lse)
    half = ring * share
    col_lse = join(col_lse, jnp.concatenate([came[:, half:], came[:, :half]], axis=1))
    for step in (1, 2, 7):
        col_lse = join_along(col_lse, RING, step)
    for axis in PLANE:
        for step in (1, 3):
            row_lse = join_along(row_lse, axis, step)

    img, mine, theirs = weights(t, s, row_lse, col_lse, srow, scol, share, ring)
    img_sent = lax.all_to_all(img.reshape(-1, share, ds), PLANE, 0, 0)
    *dealt, own = deal(mine, swap(theirs), share, ring)
    dealt = lax.optimization_barrier([turn(v, RING, k) for k, v in enumerate(dealt, 1)])
    *both, far = [v.astype(F32) for v in dealt]
    other = sum(v[share:] for v in both[1:]) + both[0][share:]
    grad_cap = own + far + sum(v[:share] for v in both[1:]) + both[0][:share] + swap(other)
    return add_up(img_sent)[None, None], grad_cap[None, None]


def solution(mesh):
    fine = Mesh(mesh.devices.reshape(2, 4, 4, 4, 2), ("zh", "x", "y", "zl", "core"))
    img = P(("zh", "x", "core"), ("y", "zl"), None, None)
    cap = P(("y", "zl"), ("zh", "x", "core"), None, None)
    return jax.shard_map(
        local,
        mesh=fine,
        in_specs=(img, cap, img, cap),
        out_specs=(img, cap),
        check_vma=False,
    )
```

```python
import math

import jax
import jax.numpy as jnp
from jax import lax
from jax.experimental import pallas as pl
from jax.experimental.pallas import tpu as pltpu
from jax.sharding import Mesh, PartitionSpec as P

LOG2E = math.log2(math.e)
teacher_scale = 0.0625 * LOG2E
student_scale = 0.125 * LOG2E
weight_scale = 0.125 * 0.5
PLANE = ("x", "y")
RING = ("zh", "zl")
BF16 = jnp.bfloat16
F32 = jnp.float32
MIB = 1024 * 1024
VMEM = pl.BlockSpec(memory_space=pltpu.VMEM)


def nt(a, b):
    return lax.dot_general(a, b, (((1,), (1,)), ((), ())), preferred_element_type=F32)


def tn(a, b):
    return lax.dot_general(a, b, (((0,), (0,)), ((), ())), preferred_element_type=F32)


def log2_sum(tile, axis):
    peak = jnp.max(tile, axis=axis, keepdims=True)
    total = jnp.sum(jnp.exp2(tile - peak), axis=axis, keepdims=True)
    return peak + jnp.log(total) * LOG2E


def join(a, b):
    return jnp.maximum(a, b) + jnp.log1p(jnp.exp2(-jnp.abs(a - b))) * LOG2E


def split(t, s, out_ref, order):
    width = t.shape[1]
    hi = t.astype(BF16)
    parts = {"high": hi, "low": (t - hi.astype(F32)).astype(BF16)}
    for i, name in enumerate(order):
        out_ref[:, i * width : (i + 1) * width] = parts[name]
    out_ref[:, 2 * width :] = s


def pack(*shards):
    share, width = shards[0].shape
    total = 2 * width + shards[1].shape[1]

    def kernel(*refs):
        sources, (rows_ref, cols_ref), (*bufs, sem) = refs[:4], refs[4:6], refs[6:]
        copies = [
            pltpu.make_async_copy(src, buf, sem.at[i])
            for i, (src, buf) in enumerate(zip(sources, bufs))
        ]
        for copy in copies:
            copy.start()
        for copy in copies:
            copy.wait()
        split(bufs[0][...], bufs[1][...], rows_ref, ("high", "low"))
        split(bufs[2][...], bufs[3][...], cols_ref, ("low", "high"))

    return pl.pallas_call(
        kernel,
        in_specs=[pl.BlockSpec(memory_space=pltpu.HBM)] * 4,
        out_specs=[VMEM] * 2,
        out_shape=[jax.ShapeDtypeStruct((share, total), BF16)] * 2,
        scratch_shapes=[pltpu.VMEM(v.shape, v.dtype) for v in shards]
        + [pltpu.SemaphoreType.DMA((4,))],
        compiler_params=pltpu.CompilerParams(vmem_limit_bytes=63 * MIB),
        name="pack",
    )(*shards)


def pair(cols, t_other, s_other):
    def kernel(cols_ref, t_ref, s_ref, out_ref):
        out_ref[0] = cols_ref[...]
        split(t_ref[...], s_ref[...], out_ref.at[1], ("low", "high"))

    return pl.pallas_call(
        kernel,
        out_shape=jax.ShapeDtypeStruct((2,) + cols.shape, BF16),
        compiler_params=pltpu.CompilerParams(vmem_limit_bytes=16 * MIB),
        name="pair",
    )(cols, t_other, s_other)


def row_plan(x, y, sign, share):
    half = share // 2

    def at(p, q, part=0):
        chip_x = lax.rem(x - sign * p + 8, 4)
        chip_y = lax.rem(y - sign * q + 8, 4)
        return (chip_x * 4 + chip_y) * share + part * half

    plan = []

    def add(piece, *parts):
        first = 0
        for p, q, part in parts:
            size = share if part is None else half
            plan.append((piece, first, size, at(p, q, part or 0)))
            first += size

    add(0, (0, 0, None))
    add(1, (1, 0, None))
    add(2, (3, 0, None))
    add(3, (0, 1, None))
    add(4, (0, 3, None))
    add(5, (2, 0, None), (1, 1, 1), (1, 3, 1))
    add(6, (3, 1, 1), (3, 3, 1))
    add(7, (0, 2, None), (1, 1, 0), (3, 1, 0))
    add(8, (1, 3, 0), (3, 3, 0))
    add(9, (2, 1, 1), (2, 3, 1), (1, 2, 1))
    add(10, (3, 2, 1))
    add(11, (1, 2, 0), (3, 2, 0), (2, 1, 0))
    add(12, (2, 3, 0))
    add(13, (2, 2, 1))
    add(14, (2, 2, 0))
    return plan


def col_plan(z, sign, share, ring):
    half = ring // 2
    plan = []
    for k in range(half):
        behind = lax.rem(z - sign * k + ring, ring) * share
        plan += [(k, 0, behind), (k, 1, ring * share + behind)]
        if k:
            ahead = lax.rem(z + sign * k + ring, ring) * share
            plan += [(half + k - 1, 1, ahead), (half + k - 1, 0, ring * share + ahead)]
    far = lax.rem(z + half, ring) * share
    plan += [(2 * half - 1, None, far), (2 * half, None, ring * share + far)]
    return plan


def logits(row_pieces, col_pieces, width, share, ring):
    m = 16 * share
    n = 2 * ring * share
    total = row_pieces[0].shape[1]
    ds = total - 2 * width
    tile = 256
    n_rows = len(row_pieces)
    n_cols = len(col_pieces)

    def kernel(*refs):
        rows_in = refs[:n_rows]
        cols_in = refs[n_rows : n_rows + n_cols]
        refs = refs[n_rows + n_cols :]
        t_ref, s_ref, row_ref, col_ref, srow_ref, scol_ref, r_buf, c_buf = refs
        x, y, z = lax.axis_index("x"), lax.axis_index("y"), lax.axis_index(RING)
        sign = 1 - 2 * lax.axis_index("core")

        def place(src, first, buf, at, size):
            def some_rows(i, _):
                there = pl.ds(pl.multiple_of(at + 32 * i, 32), 32)
                buf[there, :] = src[pl.ds(pl.multiple_of(first + 32 * i, 32), 32), :]
                return 0

            lax.fori_loop(0, size // 32, some_rows, 0)

        for piece, first, size, at in row_plan(x, y, sign, share):
            place(rows_in[piece], first, r_buf, at, size)
        for piece, part, at in col_plan(z, sign, share, ring):
            place(cols_in[piece] if part is None else cols_in[piece].at[part], 0, c_buf, at, share)

        def columns(j, _):
            here = pl.ds(pl.multiple_of(j * tile, tile), tile)
            teacher = teacher_scale * (
                nt(r_buf[:, : 2 * width], c_buf[here, : 2 * width])
                + nt(r_buf[:, :width], c_buf[here, width : 2 * width])
            )
            student = student_scale * nt(r_buf[:, 2 * width :], c_buf[here, 2 * width :])
            for k, (value, ref) in enumerate(((teacher, t_ref), (student, s_ref))):
                ref[:, here] = value
                col_ref[k : k + 1, here] = log2_sum(value, 0)
            return 0

        lax.fori_loop(0, n // tile, columns, 0, unroll=2)
        lanes = lax.broadcasted_iota(jnp.int32, (128, 128), 1)

        def row_sums(i, _):
            here = pl.ds(pl.multiple_of(i * 128, 128), 128)
            teacher = log2_sum(t_ref[here, :], 1)
            student = log2_sum(s_ref[here, :], 1)
            both = jnp.transpose(jnp.where(lanes == 0, teacher, student))
            row_ref[:, here] = both[:2, :]
            srow_ref[here, :] = r_buf[here, 2 * width :]
            scol_ref[here, :] = c_buf[here, 2 * width :]
            return 0

        lax.fori_loop(0, m // 128, row_sums, 0)

    return pl.pallas_call(
        kernel,
        in_specs=[VMEM] * (n_rows + n_cols),
        out_specs=[VMEM] * 6,
        out_shape=[
            jax.ShapeDtypeStruct((m, n), F32),
            jax.ShapeDtypeStruct((m, n), F32),
            jax.ShapeDtypeStruct((2, m), F32),
            jax.ShapeDtypeStruct((2, n), F32),
            jax.ShapeDtypeStruct((m, ds), BF16),
            jax.ShapeDtypeStruct((n, ds), BF16),
        ],
        scratch_shapes=[
            pltpu.VMEM((m, total), BF16),
            pltpu.VMEM((n, total), BF16),
        ],
        compiler_params=pltpu.CompilerParams(vmem_limit_bytes=28 * MIB),
        cost_estimate=pl.CostEstimate(
            flops=2 * m * n * (3 * width + ds),
            bytes_accessed=2 * (m + n) * total + 8 * m * n,
            transcendentals=4 * m * n,
        ),
        name="logits",
    )(*row_pieces, *col_pieces)


def weights(t, s, row_lse, col_lse, srow, scol, share, ring):
    m, n = t.shape
    ds = srow.shape[1]
    block = 256

    def kernel(
        t_ref, s_ref, row_ref, col_ref, srow_ref, scol_ref, img_ref, mine_ref, theirs_ref, *bufs
    ):
        lse, w_buf, acc = bufs
        lse[...] = jnp.transpose(jnp.concatenate([row_ref[...], jnp.zeros((126, m), F32)], axis=0))

        def some_rows(i, _):
            here = pl.ds(pl.multiple_of(i * block, block), block)
            t = t_ref[here, :]
            s = s_ref[here, :]
            row = lse[here, :]
            along_rows = jnp.exp2(s - row[:, 1:2]) - jnp.exp2(t - row[:, 0:1])
            along_cols = jnp.exp2(s - col_ref[1:2, :]) - jnp.exp2(t - col_ref[0:1, :])
            w = (weight_scale * (along_rows + along_cols)).astype(BF16)
            w_buf[here, :] = w
            img_ref[here, :] = jnp.dot(
                w, scol_ref[...], preferred_element_type=F32
            ).astype(BF16)
            return 0

        lax.fori_loop(0, m // block, some_rows, 0, unroll=2)

        def some_cols(i, _):
            here = pl.ds(pl.multiple_of(i * block, block), block)
            acc[here, :] = tn(w_buf[:, here], srow_ref[...])
            return 0

        lax.fori_loop(0, n // block, some_cols, 0)

        z = lax.axis_index(RING)
        sign = 1 - 2 * lax.axis_index("core")

        def terms(ahead, other):
            at = lax.rem(z + ahead + ring, ring) * share + other * ring * share
            return acc[pl.ds(pl.multiple_of(at, share), share), :]

        half = ring // 2
        slots = [(k, h) for k in range(1, half) for h in (0, 1)]
        for i, (k, h) in enumerate(slots):
            here = slice(i * share, (i + 1) * share)
            mine_ref[here, :] = terms(sign * k, h)
            theirs_ref[here, :] = terms(-sign * k, 1 - h)
        for i, k in enumerate((half, 0)):
            here = slice((ring - 2 + i) * share, (ring - 1 + i) * share)
            mine_ref[here, :] = terms(k, 0)
            theirs_ref[here, :] = terms(k, 1)

    return pl.pallas_call(
        kernel,
        in_specs=[VMEM] * 6,
        out_specs=[VMEM] * 3,
        out_shape=[
            jax.ShapeDtypeStruct((m, ds), BF16),
            jax.ShapeDtypeStruct((n // 2, ds), F32),
            jax.ShapeDtypeStruct((n // 2, ds), F32),
        ],
        scratch_shapes=[
            pltpu.VMEM((m, 128), F32),
            pltpu.VMEM((m, n), BF16),
            pltpu.VMEM((n, ds), F32),
        ],
        compiler_params=pltpu.CompilerParams(vmem_limit_bytes=28 * MIB),
        cost_estimate=pl.CostEstimate(
            flops=4 * m * n * ds, bytes_accessed=10 * m * n, transcendentals=4 * m * n
        ),
        name="weights",
    )(t, s, row_lse, col_lse, srow, scol)


def add_up(terms):
    def kernel(terms_ref, out_ref):
        out_ref[...] = jnp.sum(terms_ref[...].astype(F32), axis=0)

    return pl.pallas_call(
        kernel,
        out_shape=jax.ShapeDtypeStruct(terms.shape[1:], F32),
        compiler_params=pltpu.CompilerParams(vmem_limit_bytes=10 * MIB),
        name="add_up",
    )(terms)


def deal(mine, came, share, ring):
    ds = mine.shape[1]
    sizes = [2 * share] * (ring // 2 - 1) + [share]

    def kernel(mine_ref, came_ref, *out_refs):
        first = 0
        for size, ref in zip(sizes + [share], out_refs):
            here = slice(first, first + size)
            ref[...] = (mine_ref[here, :] + came_ref[here, :]).astype(ref.dtype)
            first += size

    return pl.pallas_call(
        kernel,
        in_specs=[VMEM, VMEM],
        out_specs=[VMEM] * (len(sizes) + 1),
        out_shape=[jax.ShapeDtypeStruct((size, ds), BF16) for size in sizes]
        + [jax.ShapeDtypeStruct((share, ds), F32)],
        compiler_params=pltpu.CompilerParams(vmem_limit_bytes=10 * MIB),
        name="deal",
    )(mine, came)


def swap(x):
    return lax.ppermute(x, "core", [(0, 1), (1, 0)])


def turn(x, axis, step):
    n = lax.axis_size(axis)
    axes = (axis if isinstance(axis, tuple) else (axis,)) + ("core",)
    pairs = [(2 * i + c, 2 * ((i + (step, -step)[c]) % n) + c) for i in range(n) for c in (0, 1)]
    return lax.ppermute(x, axes, pairs)


def join_along(x, axis, step):
    n = lax.axis_size(axis)
    return join(x, lax.ppermute(x, axis, [(i, i ^ step) for i in range(n)]))


def gather(r, c0, share):
    hold = lax.optimization_barrier
    half = share // 2
    a = lambda v: v[:half]
    b = lambda v: v[half : 2 * half]
    cat = lambda *v: jnp.concatenate(v, axis=0)
    x1, x1r, y1, y1r, c1 = hold(
        (turn(r, "x", 1), turn(r, "x", -1), turn(r, "y", 1), turn(r, "y", -1), turn(c0, RING, 1))
    )
    bx = cat(b(y1), b(y1r))
    ay = cat(a(x1), a(x1r))
    d1, c1 = hold((swap(c1), c1))
    x2, x2r, y2, y2r, c2, d1 = hold(
        (
            turn(cat(x1, bx), "x", 1),
            turn(bx, "x", -1),
            turn(cat(y1, ay), "y", 1),
            turn(ay, "y", -1),
            turn(c1, RING, 1),
            d1,
        )
    )
    x3, x3r, y3, y3r, c3 = hold(
        (
            turn(cat(x2[share:], b(y2)), "x", 1),
            turn(b(y2), "x", -1),
            turn(cat(y2[share:], a(x2)), "y", 1),
            turn(a(x2), "y", -1),
            turn(c2, RING, 1),
        )
    )
    x4, y4, c4, d2, d3 = hold(
        (
            turn(x3[share:], "x", 1),
            turn(y3[share:], "y", 1),
            turn(c3[0], RING, 1),
            swap(c2),
            swap(c3),
        )
    )
    rows = [r, x1, x1r, y1, y1r, x2, x2r, y2, y2r, x3, x3r, y3, y3r, x4, y4]
    return rows, [c0, c1, c2, c3, d1, d2, d3, c4, swap(c4)]


def local(teacher_img, teacher_cap, student_img, student_cap):
    width = teacher_img.shape[3]
    share, ds = student_img.shape[2:]
    ring = lax.axis_size(RING)
    came = swap(teacher_cap[0, 0]), swap(student_cap[0, 0])
    rows_own, cols_own = pack(
        teacher_img[0, 0], student_img[0, 0], teacher_cap[0, 0], student_cap[0, 0]
    )
    cols_pair = pair(cols_own, *came)
    rows, cols = gather(rows_own, cols_pair, share)
    t, s, row_lse, col_lse, srow, scol = logits(rows, cols, width, share, ring)

    came = swap(col_lse)
    half = ring * share
    col_lse = join(col_lse, jnp.concatenate([came[:, half:], came[:, :half]], axis=1))
    for step in (1, 2, 7):
        col_lse = join_along(col_lse, RING, step)
    for axis in PLANE:
        for step in (1, 3):
            row_lse = join_along(row_lse, axis, step)

    img, mine, theirs = weights(t, s, row_lse, col_lse, srow, scol, share, ring)
    img_sent = lax.all_to_all(img.reshape(-1, share, ds), PLANE, 0, 0)
    *dealt, own = deal(mine, swap(theirs), share, ring)
    dealt = lax.optimization_barrier([turn(v, RING, k) for k, v in enumerate(dealt, 1)])
    *both, far = [v.astype(F32) for v in dealt]
    other = sum(v[share:] for v in both[1:]) + both[0][share:]
    grad_cap = own + far + sum(v[:share] for v in both[1:]) + both[0][:share] + swap(other)
    return add_up(img_sent)[None, None], grad_cap[None, None]


def solution(mesh):
    fine = Mesh(mesh.devices.reshape(2, 4, 4, 4, 2), ("zh", "x", "y", "zl", "core"))
    img = P(("zh", "x", "core"), ("y", "zl"), None, None)
    cap = P(("y", "zl"), ("zh", "x", "core"), None, None)
    return jax.shard_map(
        local,
        mesh=fine,
        in_specs=(img, cap, img, cap),
        out_specs=(img, cap),
        check_vma=False,
    )
```

```python
import math

import jax
import jax.numpy as jnp
from jax import lax
from jax.experimental import pallas as pl
from jax.experimental.pallas import tpu as pltpu
from jax.sharding import Mesh, PartitionSpec as P

LOG2E = math.log2(math.e)
teacher_scale = 0.0625 * LOG2E
student_scale = 0.125 * LOG2E
weight_scale = 0.125 * 0.5
PLANE = ("x", "y")
RING = ("zh", "zl")
BF16 = jnp.bfloat16
F32 = jnp.float32
MIB = 1024 * 1024
VMEM = pl.BlockSpec(memory_space=pltpu.VMEM)


def nt(a, b):
    return lax.dot_general(a, b, (((1,), (1,)), ((), ())), preferred_element_type=F32)


def tn(a, b):
    return lax.dot_general(a, b, (((0,), (0,)), ((), ())), preferred_element_type=F32)


def log2_sum(tile, axis):
    peak = jnp.max(tile, axis=axis, keepdims=True)
    total = jnp.sum(jnp.exp2(tile - peak), axis=axis, keepdims=True)
    return peak + jnp.log(total) * LOG2E


def join(a, b):
    return jnp.maximum(a, b) + jnp.log1p(jnp.exp2(-jnp.abs(a - b))) * LOG2E


def split(t, s, out_ref, order):
    width = t.shape[1]
    hi = t.astype(BF16)
    parts = {"high": hi, "low": (t - hi.astype(F32)).astype(BF16)}
    for i, name in enumerate(order):
        out_ref[:, i * width : (i + 1) * width] = parts[name]
    out_ref[:, 2 * width :] = s


def pack(*shards):
    share, width = shards[0].shape
    total = 2 * width + shards[1].shape[1]

    def kernel(*refs):
        sources, (rows_ref, cols_ref), (*bufs, sem) = refs[:4], refs[4:6], refs[6:]
        copies = [
            pltpu.make_async_copy(src, buf, sem.at[i])
            for i, (src, buf) in enumerate(zip(sources, bufs))
        ]
        for copy in copies:
            copy.start()
        for copy in copies:
            copy.wait()
        split(bufs[0][...], bufs[1][...], rows_ref, ("high", "low"))
        split(bufs[2][...], bufs[3][...], cols_ref, ("low", "high"))

    return pl.pallas_call(
        kernel,
        in_specs=[pl.BlockSpec(memory_space=pltpu.HBM)] * 4,
        out_specs=[VMEM] * 2,
        out_shape=[jax.ShapeDtypeStruct((share, total), BF16)] * 2,
        scratch_shapes=[pltpu.VMEM(v.shape, v.dtype) for v in shards]
        + [pltpu.SemaphoreType.DMA((4,))],
        compiler_params=pltpu.CompilerParams(vmem_limit_bytes=63 * MIB),
        name="pack",
    )(*shards)


def pair(cols, t_other, s_other):
    def kernel(cols_ref, t_ref, s_ref, out_ref):
        out_ref[0] = cols_ref[...]
        split(t_ref[...], s_ref[...], out_ref.at[1], ("low", "high"))

    return pl.pallas_call(
        kernel,
        out_shape=jax.ShapeDtypeStruct((2,) + cols.shape, BF16),
        compiler_params=pltpu.CompilerParams(vmem_limit_bytes=16 * MIB),
        name="pair",
    )(cols, t_other, s_other)


def row_plan(x, y, sign, share):
    half = share // 2

    def at(p, q, part=0):
        chip_x = lax.rem(x - sign * p + 8, 4)
        chip_y = lax.rem(y - sign * q + 8, 4)
        return (chip_x * 4 + chip_y) * share + part * half

    plan = []

    def add(piece, *parts):
        first = 0
        for p, q, part in parts:
            size = share if part is None else half
            plan.append((piece, first, size, at(p, q, part or 0)))
            first += size

    add(0, (0, 0, None))
    add(1, (1, 0, None))
    add(2, (3, 0, None))
    add(3, (0, 1, None))
    add(4, (0, 3, None))
    add(5, (2, 0, None), (1, 1, 1), (1, 3, 1))
    add(6, (3, 1, 1), (3, 3, 1))
    add(7, (0, 2, None), (1, 1, 0), (3, 1, 0))
    add(8, (1, 3, 0), (3, 3, 0))
    add(9, (2, 1, 1), (2, 3, 1), (1, 2, 1))
    add(10, (3, 2, 1))
    add(11, (1, 2, 0), (3, 2, 0), (2, 1, 0))
    add(12, (2, 3, 0))
    add(13, (2, 2, 1))
    add(14, (2, 2, 0))
    return plan


def col_plan(z, sign, share, ring):
    half = ring // 2
    plan = []
    for k in range(half):
        behind = lax.rem(z - sign * k + ring, ring) * share
        plan += [(k, 0, behind), (k, 1, ring * share + behind)]
        if k:
            ahead = lax.rem(z + sign * k + ring, ring) * share
            plan += [(half + k - 1, 1, ahead), (half + k - 1, 0, ring * share + ahead)]
    far = lax.rem(z + half, ring) * share
    plan += [(2 * half - 1, None, far), (2 * half, None, ring * share + far)]
    return plan


def logits(row_pieces, col_pieces, width, share, ring):
    m = 16 * share
    n = 2 * ring * share
    total = row_pieces[0].shape[1]
    ds = total - 2 * width
    tile = 256
    n_rows = len(row_pieces)
    n_cols = len(col_pieces)

    def kernel(*refs):
        rows_in = refs[:n_rows]
        cols_in = refs[n_rows : n_rows + n_cols]
        refs = refs[n_rows + n_cols :]
        t_ref, s_ref, row_ref, col_ref, srow_ref, scol_ref, r_buf, c_buf = refs
        x, y, z = lax.axis_index("x"), lax.axis_index("y"), lax.axis_index(RING)
        sign = 1 - 2 * lax.axis_index("core")

        def place(src, first, buf, at, size):
            def some_rows(i, _):
                there = pl.ds(pl.multiple_of(at + 32 * i, 32), 32)
                buf[there, :] = src[pl.ds(pl.multiple_of(first + 32 * i, 32), 32), :]
                return 0

            lax.fori_loop(0, size // 32, some_rows, 0)

        for piece, first, size, at in row_plan(x, y, sign, share):
            place(rows_in[piece], first, r_buf, at, size)
        for piece, part, at in col_plan(z, sign, share, ring):
            place(cols_in[piece] if part is None else cols_in[piece].at[part], 0, c_buf, at, share)

        def columns(j, _):
            here = pl.ds(pl.multiple_of(j * tile, tile), tile)
            teacher = teacher_scale * (
                nt(r_buf[:, : 2 * width], c_buf[here, : 2 * width])
                + nt(r_buf[:, :width], c_buf[here, width : 2 * width])
            )
            student = student_scale * nt(r_buf[:, 2 * width :], c_buf[here, 2 * width :])
            for k, (value, ref) in enumerate(((teacher, t_ref), (student, s_ref))):
                ref[:, here] = value
                col_ref[k : k + 1, here] = log2_sum(value, 0)
            return 0

        lax.fori_loop(0, n // tile, columns, 0, unroll=2)
        lanes = lax.broadcasted_iota(jnp.int32, (128, 128), 1)

        def row_sums(i, _):
            here = pl.ds(pl.multiple_of(i * 128, 128), 128)
            teacher = log2_sum(t_ref[here, :], 1)
            student = log2_sum(s_ref[here, :], 1)
            both = jnp.transpose(jnp.where(lanes == 0, teacher, student))
            row_ref[:, here] = both[:2, :]
            srow_ref[here, :] = r_buf[here, 2 * width :]
            scol_ref[here, :] = c_buf[here, 2 * width :]
            return 0

        lax.fori_loop(0, m // 128, row_sums, 0, unroll=4)

    return pl.pallas_call(
        kernel,
        in_specs=[VMEM] * (n_rows + n_cols),
        out_specs=[VMEM] * 6,
        out_shape=[
            jax.ShapeDtypeStruct((m, n), F32),
            jax.ShapeDtypeStruct((m, n), F32),
            jax.ShapeDtypeStruct((2, m), F32),
            jax.ShapeDtypeStruct((2, n), F32),
            jax.ShapeDtypeStruct((m, ds), BF16),
            jax.ShapeDtypeStruct((n, ds), BF16),
        ],
        scratch_shapes=[
            pltpu.VMEM((m, total), BF16),
            pltpu.VMEM((n, total), BF16),
        ],
        compiler_params=pltpu.CompilerParams(vmem_limit_bytes=28 * MIB),
        cost_estimate=pl.CostEstimate(
            flops=2 * m * n * (3 * width + ds),
            bytes_accessed=2 * (m + n) * total + 8 * m * n,
            transcendentals=4 * m * n,
        ),
        name="logits",
    )(*row_pieces, *col_pieces)


def weights(t, s, row_lse, col_lse, srow, scol, share, ring):
    m, n = t.shape
    ds = srow.shape[1]
    block = 256

    def kernel(
        t_ref, s_ref, row_ref, col_ref, srow_ref, scol_ref, img_ref, mine_ref, theirs_ref, *bufs
    ):
        lse, w_buf, acc = bufs
        lse[...] = jnp.transpose(jnp.concatenate([row_ref[...], jnp.zeros((126, m), F32)], axis=0))

        def some_rows(i, _):
            here = pl.ds(pl.multiple_of(i * block, block), block)
            t = t_ref[here, :]
            s = s_ref[here, :]
            row = lse[here, :]
            along_rows = jnp.exp2(s - row[:, 1:2]) - jnp.exp2(t - row[:, 0:1])
            along_cols = jnp.exp2(s - col_ref[1:2, :]) - jnp.exp2(t - col_ref[0:1, :])
            w = (weight_scale * (along_rows + along_cols)).astype(BF16)
            w_buf[here, :] = w
            img_ref[here, :] = jnp.dot(
                w, scol_ref[...], preferred_element_type=F32
            ).astype(BF16)
            return 0

        lax.fori_loop(0, m // block, some_rows, 0, unroll=2)

        def some_cols(i, _):
            here = pl.ds(pl.multiple_of(i * block, block), block)
            acc[here, :] = tn(w_buf[:, here], srow_ref[...])
            return 0

        lax.fori_loop(0, n // block, some_cols, 0, unroll=2)

        z = lax.axis_index(RING)
        sign = 1 - 2 * lax.axis_index("core")

        def terms(ahead, other):
            at = lax.rem(z + ahead + ring, ring) * share + other * ring * share
            return acc[pl.ds(pl.multiple_of(at, share), share), :]

        half = ring // 2
        slots = [(k, h) for k in range(1, half) for h in (0, 1)]
        for i, (k, h) in enumerate(slots):
            here = slice(i * share, (i + 1) * share)
            mine_ref[here, :] = terms(sign * k, h)
            theirs_ref[here, :] = terms(-sign * k, 1 - h)
        for i, k in enumerate((half, 0)):
            here = slice((ring - 2 + i) * share, (ring - 1 + i) * share)
            mine_ref[here, :] = terms(k, 0)
            theirs_ref[here, :] = terms(k, 1)

    return pl.pallas_call(
        kernel,
        in_specs=[VMEM] * 6,
        out_specs=[VMEM] * 3,
        out_shape=[
            jax.ShapeDtypeStruct((m, ds), BF16),
            jax.ShapeDtypeStruct((n // 2, ds), F32),
            jax.ShapeDtypeStruct((n // 2, ds), F32),
        ],
        scratch_shapes=[
            pltpu.VMEM((m, 128), F32),
            pltpu.VMEM((m, n), BF16),
            pltpu.VMEM((n, ds), F32),
        ],
        compiler_params=pltpu.CompilerParams(vmem_limit_bytes=28 * MIB),
        cost_estimate=pl.CostEstimate(
            flops=4 * m * n * ds, bytes_accessed=10 * m * n, transcendentals=4 * m * n
        ),
        name="weights",
    )(t, s, row_lse, col_lse, srow, scol)


def add_up(terms):
    def kernel(terms_ref, out_ref):
        out_ref[...] = jnp.sum(terms_ref[...].astype(F32), axis=0)

    return pl.pallas_call(
        kernel,
        out_shape=jax.ShapeDtypeStruct(terms.shape[1:], F32),
        compiler_params=pltpu.CompilerParams(vmem_limit_bytes=10 * MIB),
        name="add_up",
    )(terms)


def deal(mine, came, share, ring):
    ds = mine.shape[1]
    sizes = [2 * share] * (ring // 2 - 1) + [share]

    def kernel(mine_ref, came_ref, *out_refs):
        first = 0
        for size, ref in zip(sizes + [share], out_refs):
            here = slice(first, first + size)
            ref[...] = (mine_ref[here, :] + came_ref[here, :]).astype(ref.dtype)
            first += size

    return pl.pallas_call(
        kernel,
        in_specs=[VMEM, VMEM],
        out_specs=[VMEM] * (len(sizes) + 1),
        out_shape=[jax.ShapeDtypeStruct((size, ds), BF16) for size in sizes]
        + [jax.ShapeDtypeStruct((share, ds), F32)],
        compiler_params=pltpu.CompilerParams(vmem_limit_bytes=10 * MIB),
        name="deal",
    )(mine, came)


def swap(x):
    return lax.ppermute(x, "core", [(0, 1), (1, 0)])


def turn(x, axis, step):
    n = lax.axis_size(axis)
    axes = (axis if isinstance(axis, tuple) else (axis,)) + ("core",)
    pairs = [(2 * i + c, 2 * ((i + (step, -step)[c]) % n) + c) for i in range(n) for c in (0, 1)]
    return lax.ppermute(x, axes, pairs)


def join_along(x, axis, step):
    n = lax.axis_size(axis)
    return join(x, lax.ppermute(x, axis, [(i, i ^ step) for i in range(n)]))


def gather(r, c0, share):
    hold = lax.optimization_barrier
    half = share // 2
    a = lambda v: v[:half]
    b = lambda v: v[half : 2 * half]
    cat = lambda *v: jnp.concatenate(v, axis=0)
    x1, x1r, y1, y1r, c1 = hold(
        (turn(r, "x", 1), turn(r, "x", -1), turn(r, "y", 1), turn(r, "y", -1), turn(c0, RING, 1))
    )
    bx = cat(b(y1), b(y1r))
    ay = cat(a(x1), a(x1r))
    d1, c1 = hold((swap(c1), c1))
    x2, x2r, y2, y2r, c2, d1 = hold(
        (
            turn(cat(x1, bx), "x", 1),
            turn(bx, "x", -1),
            turn(cat(y1, ay), "y", 1),
            turn(ay, "y", -1),
            turn(c1, RING, 1),
            d1,
        )
    )
    x3, x3r, y3, y3r, c3 = hold(
        (
            turn(cat(x2[share:], b(y2)), "x", 1),
            turn(b(y2), "x", -1),
            turn(cat(y2[share:], a(x2)), "y", 1),
            turn(a(x2), "y", -1),
            turn(c2, RING, 1),
        )
    )
    x4, y4, c4, d2, d3 = hold(
        (
            turn(x3[share:], "x", 1),
            turn(y3[share:], "y", 1),
            turn(c3[0], RING, 1),
            swap(c2),
            swap(c3),
        )
    )
    rows = [r, x1, x1r, y1, y1r, x2, x2r, y2, y2r, x3, x3r, y3, y3r, x4, y4]
    return rows, [c0, c1, c2, c3, d1, d2, d3, c4, swap(c4)]


def local(teacher_img, teacher_cap, student_img, student_cap):
    width = teacher_img.shape[3]
    share, ds = student_img.shape[2:]
    ring = lax.axis_size(RING)
    came = swap(teacher_cap[0, 0]), swap(student_cap[0, 0])
    rows_own, cols_own = pack(
        teacher_img[0, 0], student_img[0, 0], teacher_cap[0, 0], student_cap[0, 0]
    )
    cols_pair = pair(cols_own, *came)
    rows, cols = gather(rows_own, cols_pair, share)
    t, s, row_lse, col_lse, srow, scol = logits(rows, cols, width, share, ring)

    came = swap(col_lse)
    half = ring * share
    col_lse = join(col_lse, jnp.concatenate([came[:, half:], came[:, :half]], axis=1))
    for step in (1, 2, 7):
        col_lse = join_along(col_lse, RING, step)
    for axis in PLANE:
        for step in (1, 3):
            row_lse = join_along(row_lse, axis, step)

    img, mine, theirs = weights(t, s, row_lse, col_lse, srow, scol, share, ring)
    img_sent = lax.all_to_all(img.reshape(-1, share, ds), PLANE, 0, 0)
    *dealt, own = deal(mine, swap(theirs), share, ring)
    dealt = lax.optimization_barrier([turn(v, RING, k) for k, v in enumerate(dealt, 1)])
    *both, far = [v.astype(F32) for v in dealt]
    other = sum(v[share:] for v in both[1:]) + both[0][share:]
    grad_cap = own + far + sum(v[:share] for v in both[1:]) + both[0][:share] + swap(other)
    return add_up(img_sent)[None, None], grad_cap[None, None]


def solution(mesh):
    fine = Mesh(mesh.devices.reshape(2, 4, 4, 4, 2), ("zh", "x", "y", "zl", "core"))
    img = P(("zh", "x", "core"), ("y", "zl"), None, None)
    cap = P(("y", "zl"), ("zh", "x", "core"), None, None)
    return jax.shard_map(
        local,
        mesh=fine,
        in_specs=(img, cap, img, cap),
        out_specs=(img, cap),
        check_vma=False,
    )
```

```python
import math

import jax
import jax.numpy as jnp
from jax import lax
from jax.experimental import pallas as pl
from jax.experimental.pallas import tpu as pltpu
from jax.sharding import Mesh, PartitionSpec as P

LOG2E = math.log2(math.e)
teacher_scale = 0.0625 * LOG2E
student_scale = 0.125 * LOG2E
weight_scale = 0.125 * 0.5
PLANE = ("x", "y")
RING = ("zh", "zl")
BF16 = jnp.bfloat16
F32 = jnp.float32
MIB = 1024 * 1024
VMEM = pl.BlockSpec(memory_space=pltpu.VMEM)


def nt(a, b):
    return lax.dot_general(a, b, (((1,), (1,)), ((), ())), preferred_element_type=F32)


def tn(a, b):
    return lax.dot_general(a, b, (((0,), (0,)), ((), ())), preferred_element_type=F32)


def log2_sum(tile, axis):
    peak = jnp.max(tile, axis=axis, keepdims=True)
    total = jnp.sum(jnp.exp2(tile - peak), axis=axis, keepdims=True)
    return peak + jnp.log(total) * LOG2E


def join(a, b):
    return jnp.maximum(a, b) + jnp.log1p(jnp.exp2(-jnp.abs(a - b))) * LOG2E


def split(t, s, out_ref, order):
    width = t.shape[1]
    hi = t.astype(BF16)
    parts = {"high": hi, "low": (t - hi.astype(F32)).astype(BF16)}
    for i, name in enumerate(order):
        out_ref[:, i * width : (i + 1) * width] = parts[name]
    out_ref[:, 2 * width :] = s


def pack(*shards):
    share, width = shards[0].shape
    total = 2 * width + shards[1].shape[1]

    def kernel(*refs):
        sources, (rows_ref, cols_ref), (*bufs, sem) = refs[:4], refs[4:6], refs[6:]
        copies = [
            pltpu.make_async_copy(src, buf, sem.at[i])
            for i, (src, buf) in enumerate(zip(sources, bufs))
        ]
        for copy in copies:
            copy.start()
        for copy in copies:
            copy.wait()
        split(bufs[0][...], bufs[1][...], rows_ref, ("high", "low"))
        split(bufs[2][...], bufs[3][...], cols_ref, ("low", "high"))

    return pl.pallas_call(
        kernel,
        in_specs=[pl.BlockSpec(memory_space=pltpu.HBM)] * 4,
        out_specs=[VMEM] * 2,
        out_shape=[jax.ShapeDtypeStruct((share, total), BF16)] * 2,
        scratch_shapes=[pltpu.VMEM(v.shape, v.dtype) for v in shards]
        + [pltpu.SemaphoreType.DMA((4,))],
        compiler_params=pltpu.CompilerParams(vmem_limit_bytes=63 * MIB),
        name="pack",
    )(*shards)


def pair(cols, t_other, s_other):
    def kernel(cols_ref, t_ref, s_ref, out_ref):
        out_ref[0] = cols_ref[...]
        split(t_ref[...], s_ref[...], out_ref.at[1], ("low", "high"))

    return pl.pallas_call(
        kernel,
        out_shape=jax.ShapeDtypeStruct((2,) + cols.shape, BF16),
        compiler_params=pltpu.CompilerParams(vmem_limit_bytes=16 * MIB),
        name="pair",
    )(cols, t_other, s_other)


def row_plan(x, y, sign, share):
    half = share // 2

    def at(p, q, part=0):
        chip_x = lax.rem(x - sign * p + 8, 4)
        chip_y = lax.rem(y - sign * q + 8, 4)
        return (chip_x * 4 + chip_y) * share + part * half

    plan = []

    def add(piece, *parts):
        first = 0
        for p, q, part in parts:
            size = share if part is None else half
            plan.append((piece, first, size, at(p, q, part or 0)))
            first += size

    add(0, (0, 0, None))
    add(1, (1, 0, None))
    add(2, (3, 0, None))
    add(3, (0, 1, None))
    add(4, (0, 3, None))
    add(5, (2, 0, None), (1, 1, 1), (1, 3, 1))
    add(6, (3, 1, 1), (3, 3, 1))
    add(7, (0, 2, None), (1, 1, 0), (3, 1, 0))
    add(8, (1, 3, 0), (3, 3, 0))
    add(9, (2, 1, 1), (2, 3, 1), (1, 2, 1))
    add(10, (3, 2, 1))
    add(11, (1, 2, 0), (3, 2, 0), (2, 1, 0))
    add(12, (2, 3, 0))
    add(13, (2, 2, 1))
    add(14, (2, 2, 0))
    return plan


def col_plan(z, sign, share, ring):
    half = ring // 2
    plan = []
    for k in range(half):
        behind = lax.rem(z - sign * k + ring, ring) * share
        plan += [(k, 0, behind), (k, 1, ring * share + behind)]
        if k:
            ahead = lax.rem(z + sign * k + ring, ring) * share
            plan += [(half + k - 1, 1, ahead), (half + k - 1, 0, ring * share + ahead)]
    far = lax.rem(z + half, ring) * share
    plan += [(2 * half - 1, None, far), (2 * half, None, ring * share + far)]
    return plan


def logits(row_pieces, col_pieces, width, share, ring):
    m = 16 * share
    n = 2 * ring * share
    total = row_pieces[0].shape[1]
    ds = total - 2 * width
    tile = 256
    n_rows = len(row_pieces)
    n_cols = len(col_pieces)

    def kernel(*refs):
        rows_in = refs[:n_rows]
        cols_in = refs[n_rows : n_rows + n_cols]
        refs = refs[n_rows + n_cols :]
        t_ref, s_ref, row_ref, col_ref, srow_ref, scol_ref, r_buf, c_buf = refs
        x, y, z = lax.axis_index("x"), lax.axis_index("y"), lax.axis_index(RING)
        sign = 1 - 2 * lax.axis_index("core")

        def place(src, first, buf, at, size):
            def some_rows(i, _):
                there = pl.ds(pl.multiple_of(at + 32 * i, 32), 32)
                buf[there, :] = src[pl.ds(pl.multiple_of(first + 32 * i, 32), 32), :]
                return 0

            lax.fori_loop(0, size // 32, some_rows, 0)

        for piece, first, size, at in row_plan(x, y, sign, share):
            place(rows_in[piece], first, r_buf, at, size)
        for piece, part, at in col_plan(z, sign, share, ring):
            place(cols_in[piece] if part is None else cols_in[piece].at[part], 0, c_buf, at, share)

        def columns(j, _):
            here = pl.ds(pl.multiple_of(j * tile, tile), tile)
            teacher = teacher_scale * (
                nt(r_buf[:, : 2 * width], c_buf[here, : 2 * width])
                + nt(r_buf[:, :width], c_buf[here, width : 2 * width])
            )
            student = student_scale * nt(r_buf[:, 2 * width :], c_buf[here, 2 * width :])
            for k, (value, ref) in enumerate(((teacher, t_ref), (student, s_ref))):
                ref[:, here] = value
                col_ref[k : k + 1, here] = log2_sum(value, 0)
            return 0

        lax.fori_loop(0, n // tile, columns, 0, unroll=2)
        lanes = lax.broadcasted_iota(jnp.int32, (128, 128), 1)

        def row_sums(i, _):
            here = pl.ds(pl.multiple_of(i * 128, 128), 128)
            teacher = log2_sum(t_ref[here, :], 1)
            student = log2_sum(s_ref[here, :], 1)
            both = jnp.transpose(jnp.where(lanes == 0, teacher, student))
            row_ref[:, here] = both[:2, :]
            srow_ref[here, :] = r_buf[here, 2 * width :]
            scol_ref[here, :] = c_buf[here, 2 * width :]
            return 0

        lax.fori_loop(0, m // 128, row_sums, 0, unroll=8)

    return pl.pallas_call(
        kernel,
        in_specs=[VMEM] * (n_rows + n_cols),
        out_specs=[VMEM] * 6,
        out_shape=[
            jax.ShapeDtypeStruct((m, n), F32),
            jax.ShapeDtypeStruct((m, n), F32),
            jax.ShapeDtypeStruct((2, m), F32),
            jax.ShapeDtypeStruct((2, n), F32),
            jax.ShapeDtypeStruct((m, ds), BF16),
            jax.ShapeDtypeStruct((n, ds), BF16),
        ],
        scratch_shapes=[
            pltpu.VMEM((m, total), BF16),
            pltpu.VMEM((n, total), BF16),
        ],
        compiler_params=pltpu.CompilerParams(vmem_limit_bytes=28 * MIB),
        cost_estimate=pl.CostEstimate(
            flops=2 * m * n * (3 * width + ds),
            bytes_accessed=2 * (m + n) * total + 8 * m * n,
            transcendentals=4 * m * n,
        ),
        name="logits",
    )(*row_pieces, *col_pieces)


def weights(t, s, row_lse, col_lse, srow, scol, share, ring):
    m, n = t.shape
    ds = srow.shape[1]
    block = 256

    def kernel(
        t_ref, s_ref, row_ref, col_ref, srow_ref, scol_ref, img_ref, mine_ref, theirs_ref, *bufs
    ):
        lse, w_buf, acc = bufs
        lse[...] = jnp.transpose(jnp.concatenate([row_ref[...], jnp.zeros((126, m), F32)], axis=0))

        def some_rows(i, _):
            here = pl.ds(pl.multiple_of(i * block, block), block)
            t = t_ref[here, :]
            s = s_ref[here, :]
            row = lse[here, :]
            along_rows = jnp.exp2(s - row[:, 1:2]) - jnp.exp2(t - row[:, 0:1])
            along_cols = jnp.exp2(s - col_ref[1:2, :]) - jnp.exp2(t - col_ref[0:1, :])
            w = (weight_scale * (along_rows + along_cols)).astype(BF16)
            w_buf[here, :] = w
            img_ref[here, :] = jnp.dot(
                w, scol_ref[...], preferred_element_type=F32
            ).astype(BF16)
            return 0

        lax.fori_loop(0, m // block, some_rows, 0, unroll=2)

        def some_cols(i, _):
            here = pl.ds(pl.multiple_of(i * block, block), block)
            acc[here, :] = tn(w_buf[:, here], srow_ref[...])
            return 0

        lax.fori_loop(0, n // block, some_cols, 0, unroll=4)

        z = lax.axis_index(RING)
        sign = 1 - 2 * lax.axis_index("core")

        def terms(ahead, other):
            at = lax.rem(z + ahead + ring, ring) * share + other * ring * share
            return acc[pl.ds(pl.multiple_of(at, share), share), :]

        half = ring // 2
        slots = [(k, h) for k in range(1, half) for h in (0, 1)]
        for i, (k, h) in enumerate(slots):
            here = slice(i * share, (i + 1) * share)
            mine_ref[here, :] = terms(sign * k, h)
            theirs_ref[here, :] = terms(-sign * k, 1 - h)
        for i, k in enumerate((half, 0)):
            here = slice((ring - 2 + i) * share, (ring - 1 + i) * share)
            mine_ref[here, :] = terms(k, 0)
            theirs_ref[here, :] = terms(k, 1)

    return pl.pallas_call(
        kernel,
        in_specs=[VMEM] * 6,
        out_specs=[VMEM] * 3,
        out_shape=[
            jax.ShapeDtypeStruct((m, ds), BF16),
            jax.ShapeDtypeStruct((n // 2, ds), F32),
            jax.ShapeDtypeStruct((n // 2, ds), F32),
        ],
        scratch_shapes=[
            pltpu.VMEM((m, 128), F32),
            pltpu.VMEM((m, n), BF16),
            pltpu.VMEM((n, ds), F32),
        ],
        compiler_params=pltpu.CompilerParams(vmem_limit_bytes=28 * MIB),
        cost_estimate=pl.CostEstimate(
            flops=4 * m * n * ds, bytes_accessed=10 * m * n, transcendentals=4 * m * n
        ),
        name="weights",
    )(t, s, row_lse, col_lse, srow, scol)


def add_up(terms):
    def kernel(terms_ref, out_ref):
        out_ref[...] = jnp.sum(terms_ref[...].astype(F32), axis=0)

    return pl.pallas_call(
        kernel,
        out_shape=jax.ShapeDtypeStruct(terms.shape[1:], F32),
        compiler_params=pltpu.CompilerParams(vmem_limit_bytes=10 * MIB),
        name="add_up",
    )(terms)


def deal(mine, came, share, ring):
    ds = mine.shape[1]
    sizes = [2 * share] * (ring // 2 - 1) + [share]

    def kernel(mine_ref, came_ref, *out_refs):
        first = 0
        for size, ref in zip(sizes + [share], out_refs):
            here = slice(first, first + size)
            ref[...] = (mine_ref[here, :] + came_ref[here, :]).astype(ref.dtype)
            first += size

    return pl.pallas_call(
        kernel,
        in_specs=[VMEM, VMEM],
        out_specs=[VMEM] * (len(sizes) + 1),
        out_shape=[jax.ShapeDtypeStruct((size, ds), BF16) for size in sizes]
        + [jax.ShapeDtypeStruct((share, ds), F32)],
        compiler_params=pltpu.CompilerParams(vmem_limit_bytes=10 * MIB),
        name="deal",
    )(mine, came)


def swap(x):
    return lax.ppermute(x, "core", [(0, 1), (1, 0)])


def turn(x, axis, step):
    n = lax.axis_size(axis)
    axes = (axis if isinstance(axis, tuple) else (axis,)) + ("core",)
    pairs = [(2 * i + c, 2 * ((i + (step, -step)[c]) % n) + c) for i in range(n) for c in (0, 1)]
    return lax.ppermute(x, axes, pairs)


def join_along(x, axis, step):
    n = lax.axis_size(axis)
    return join(x, lax.ppermute(x, axis, [(i, i ^ step) for i in range(n)]))


def gather(r, c0, share):
    hold = lax.optimization_barrier
    half = share // 2
    a = lambda v: v[:half]
    b = lambda v: v[half : 2 * half]
    cat = lambda *v: jnp.concatenate(v, axis=0)
    x1, x1r, y1, y1r, c1 = hold(
        (turn(r, "x", 1), turn(r, "x", -1), turn(r, "y", 1), turn(r, "y", -1), turn(c0, RING, 1))
    )
    bx = cat(b(y1), b(y1r))
    ay = cat(a(x1), a(x1r))
    d1, c1 = hold((swap(c1), c1))
    x2, x2r, y2, y2r, c2, d1 = hold(
        (
            turn(cat(x1, bx), "x", 1),
            turn(bx, "x", -1),
            turn(cat(y1, ay), "y", 1),
            turn(ay, "y", -1),
            turn(c1, RING, 1),
            d1,
        )
    )
    x3, x3r, y3, y3r, c3 = hold(
        (
            turn(cat(x2[share:], b(y2)), "x", 1),
            turn(b(y2), "x", -1),
            turn(cat(y2[share:], a(x2)), "y", 1),
            turn(a(x2), "y", -1),
            turn(c2, RING, 1),
        )
    )
    x4, y4, c4, d2, d3 = hold(
        (
            turn(x3[share:], "x", 1),
            turn(y3[share:], "y", 1),
            turn(c3[0], RING, 1),
            swap(c2),
            swap(c3),
        )
    )
    rows = [r, x1, x1r, y1, y1r, x2, x2r, y2, y2r, x3, x3r, y3, y3r, x4, y4]
    return rows, [c0, c1, c2, c3, d1, d2, d3, c4, swap(c4)]


def local(teacher_img, teacher_cap, student_img, student_cap):
    width = teacher_img.shape[3]
    share, ds = student_img.shape[2:]
    ring = lax.axis_size(RING)
    came = swap(teacher_cap[0, 0]), swap(student_cap[0, 0])
    rows_own, cols_own = pack(
        teacher_img[0, 0], student_img[0, 0], teacher_cap[0, 0], student_cap[0, 0]
    )
    cols_pair = pair(cols_own, *came)
    rows, cols = gather(rows_own, cols_pair, share)
    t, s, row_lse, col_lse, srow, scol = logits(rows, cols, width, share, ring)

    came = swap(col_lse)
    half = ring * share
    col_lse = join(col_lse, jnp.concatenate([came[:, half:], came[:, :half]], axis=1))
    for step in (1, 2, 7):
        col_lse = join_along(col_lse, RING, step)
    for axis in PLANE:
        for step in (1, 3):
            row_lse = join_along(row_lse, axis, step)

    img, mine, theirs = weights(t, s, row_lse, col_lse, srow, scol, share, ring)
    img_sent = lax.all_to_all(img.reshape(-1, share, ds), PLANE, 0, 0)
    *dealt, own = deal(mine, swap(theirs), share, ring)
    dealt = lax.optimization_barrier([turn(v, RING, k) for k, v in enumerate(dealt, 1)])
    *both, far = [v.astype(F32) for v in dealt]
    other = sum(v[share:] for v in both[1:]) + both[0][share:]
    grad_cap = own + far + sum(v[:share] for v in both[1:]) + both[0][:share] + swap(other)
    return add_up(img_sent)[None, None], grad_cap[None, None]


def solution(mesh):
    fine = Mesh(mesh.devices.reshape(2, 4, 4, 4, 2), ("zh", "x", "y", "zl", "core"))
    img = P(("zh", "x", "core"), ("y", "zl"), None, None)
    cap = P(("y", "zl"), ("zh", "x", "core"), None, None)
    return jax.shard_map(
        local,
        mesh=fine,
        in_specs=(img, cap, img, cap),
        out_specs=(img, cap),
        check_vma=False,
    )
```
